512 devices in a mesh: tok: 16 (over x_hi, y, core), atom: 32 (over z, x_lo).
Axes of the slice: x: 4 (x_hi: 2, x_lo: 2; x = x_hi * 2 + x_lo), y: 4, z: 16, core: 2. Of those that a mesh axis runs over, the one named last changes fastest.
Arguments:
- atoms: bfloat16 [655360, 128], P(('tok', 'atom')), may hold values from -6 to 6
- atom_bias: bfloat16 [655360, 4, 128], P(('tok', 'atom')), may hold values from -400 to 400
- atom_token: int32 [655360], P(('tok', 'atom')), may hold values from 0 to 4095, as said below
- token_atoms: int32 [65536], P(('tok', 'atom')), may hold values from 1 to 1793, as said below
- token_single: bfloat16 [65536, 768], P(('tok', 'atom')), may hold values from -6 to 6
- key_value: bfloat16 [2, 64, 768], P(None, 'tok'), may hold values from -6 to 6
- pair: bfloat16 [65536, 64, 128], P(('tok', 'atom')), may hold values from -600 to 600
- atom_gain: float32 [128], replicated, may hold values from 0.1 to 1.9
- atom_qkv: bfloat16 [128, 384], replicated, may hold values from -0.5 to 0.5
- atom_out_weight: bfloat16 [128, 128], replicated, may hold values from -0.5 to 0.5
- agg_weight: bfloat16 [128, 768], replicated, may hold values from -0.5 to 0.5
- token_gain: float32 [768], replicated, may hold values from 0.1 to 1.9
- query_gate_weight: bfloat16 [2, 768, 768], P(None, None, 'tok'), may hold values from -0.625 to 0.625
- pair_weight: bfloat16 [128, 16], replicated, may hold values from -0.5 to 0.5
- out_weight: bfloat16 [768, 768], P('tok'), may hold values from -0.21875 to 0.21875
Outputs:
- atom_update: bfloat16 [655360, 128], P(('tok', 'atom'))
- token_update: bfloat16 [65536, 768], P(('tok', 'atom'))
The draws below stay inside these ranges and needn't reach their ends.
Inputs may be any that keep to these rules, and one draw needn't show every extreme that they name: `atom_token`: within each group the atoms belong to the group's tokens in non-decreasing order, token u of the group having token_atoms of it atoms; atom r of a group belongs to a token u with |r // 1280 - u // 128| <= 1. `token_atoms`: the counts of a group sum to 40960.
All inputs are finite; a program needn't handle non-finite values.
Results may differ from the reference program's by a relative error of at most 0.014.
Values may be sent and summed in bfloat16 or wider, within the bound.
A program may use at most 64 MiB of HBM per device.

```python
import jax
import jax.numpy as jnp
from jax import lax

C_ATOM = 128
ATOM_HEADS = 4
C_TOKEN = 768
HEADS = 16
PAIR = 128
QWIN = 32
KWIN = 128
RIM = 48
TOK_DEV = 128
ATOM_DEV = 1280
GROUP_TOKENS = 4096
GROUP_ATOMS = 40960
TOKENS = 65536
ATOMS = 655360
KEYS = 64


def shared_counts(key):
    key = jax.random.fold_in(key, 11)
    first_key, second_key = jax.random.split(key)
    groups = TOKENS // GROUP_TOKENS
    owners = GROUP_TOKENS // TOK_DEV
    quarter = ATOM_DEV // 4
    shifted = jax.random.randint(first_key, (groups, owners), -quarter, quarter + 1)
    shifted = shifted.at[0, 0].set(-quarter)
    shifted = shifted.at[0, 1].set(quarter)
    shifted = shifted.at[:, owners - 1].set(0)
    before = jnp.concatenate([jnp.zeros((groups, 1), jnp.int32), shifted[:, :-1]], axis=1)
    owner_totals = ATOM_DEV + shifted - before
    spare = owner_totals - TOK_DEV
    weights = jax.random.randint(second_key, (groups, owners, TOK_DEV), 1, 9)
    single = jnp.where(jnp.arange(TOK_DEV) == 0, 1, 0).astype(weights.dtype)
    weights = weights.at[0, 1, :].set(single)
    running = jnp.cumsum(weights, axis=2)
    whole = running[:, :, -1:]
    ends = spare[:, :, None] * running // whole
    starts = jnp.concatenate([jnp.zeros((groups, owners, 1), jnp.int32), ends[:, :, :-1]], axis=2)
    counts = 1 + ends - starts
    return counts.reshape(groups, GROUP_TOKENS).astype(jnp.int32)


def draw_token_atoms(key, part):
    counts = shared_counts(key)
    return counts.reshape(TOKENS)


def draw_atom_token(key, part):
    counts = shared_counts(key)
    ends = jnp.cumsum(counts, axis=1)
    places = jnp.arange(GROUP_ATOMS, dtype=jnp.int32)
    tokens = jax.vmap(lambda bounds: jnp.searchsorted(bounds, places, side='right'))(ends)
    return tokens.astype(jnp.int32).reshape(ATOMS)


def draw_atom_bias(key, part):
    key = jax.random.fold_in(key, 3)
    keys = jax.random.split(key, 1)
    shape = (ATOMS, ATOM_HEADS, KWIN)
    return jnp.clip(jax.random.normal(keys[0], shape, jnp.float32), -6.0, 6.0).astype(jnp.bfloat16)


def draw_pair(key, part):
    key = jax.random.fold_in(key, 4)
    keys = jax.random.split(key, 1)
    shape = (TOKENS, KEYS, PAIR)
    return jnp.clip(jax.random.normal(keys[0], shape, jnp.float32), -6.0, 6.0).astype(jnp.bfloat16)


def steps_of(own_key, extent, shards, least, top_value):
    def one(position, parts):
        draws = jax.random.uniform(jax.random.fold_in(jax.random.fold_in(own_key, 6), position), (parts,), jnp.float32, least / len(shards), top_value / len(shards))
        return jnp.repeat(jnp.exp(draws), extent[position] // parts).reshape((-1,) + (1,) * (len(extent) - position - 1))

    factor_of = one(*shards[0])
    for cut in shards[1:]:
        factor_of = factor_of * one(*cut)
    return factor_of


def gaussian(rng, dims, deviation, reach, pieces=(), kind=jnp.bfloat16):
    array = deviation * jax.random.normal(rng, dims, jnp.float32)
    if pieces:
        array = array * steps_of(rng, dims, pieces, -0.22, 0.18)
    return jnp.clip(array, -reach, reach).astype(kind)


def setup_inputs(seed: int = 0) -> dict:
    key_list = jax.random.split(jax.random.key(seed), 16)
    atoms = gaussian(key_list[0], (ATOMS, C_ATOM), 1.0, 6.0, ((0, 512),))
    atom_bias = draw_atom_bias(jax.random.fold_in(key_list[15], 71), 0)
    atom_token = draw_atom_token(jax.random.fold_in(key_list[15], 71), 0)
    token_atoms = draw_token_atoms(jax.random.fold_in(key_list[15], 71), 0)
    token_single = gaussian(key_list[4], (TOKENS, C_TOKEN), 1.0, 6.0, ((0, 512),))
    key_value = gaussian(key_list[5], (2, KEYS, C_TOKEN), 1.0, 6.0, ((1, 16),))
    pair = draw_pair(jax.random.fold_in(key_list[15], 71), 0)
    atom_gain = jnp.clip(1.0 + 0.18 * jax.random.normal(key_list[7], (C_ATOM,), jnp.float32), 0.1, 1.9)
    atom_qkv = gaussian(key_list[8], (C_ATOM, 3 * C_ATOM), C_ATOM ** -0.5, 0.5)
    atom_out_weight = gaussian(key_list[9], (C_ATOM, C_ATOM), C_ATOM ** -0.5, 0.5)
    agg_weight = gaussian(key_list[10], (C_ATOM, C_TOKEN), C_ATOM ** -0.5, 0.5)
    token_gain = jnp.clip(1.0 + 0.18 * jax.random.normal(key_list[11], (C_TOKEN,), jnp.float32), 0.1, 1.9)
    query_gate_weight = gaussian(key_list[12], (2, C_TOKEN, C_TOKEN), (C_TOKEN // 8) ** -0.5, 0.625, ((2, 16),))
    pair_weight = gaussian(key_list[13], (PAIR, HEADS), PAIR ** -0.5, 0.5)
    out_weight = gaussian(key_list[14], (C_TOKEN, C_TOKEN), C_TOKEN ** -0.5, 0.21875, ((0, 16),))
    return {"atoms": atoms, "atom_bias": atom_bias, "atom_token": atom_token, "token_atoms": token_atoms, "token_single": token_single, "key_value": key_value, "pair": pair, "atom_gain": atom_gain, "atom_qkv": atom_qkv, "atom_out_weight": atom_out_weight, "agg_weight": agg_weight, "token_gain": token_gain, "query_gate_weight": query_gate_weight, "pair_weight": pair_weight, "out_weight": out_weight}


EPSILON = 1e-05

def layer_norm(values, gain):
    centre = values - lax.optimization_barrier(jnp.mean(values, axis=-1, keepdims=True))
    spread = lax.optimization_barrier(jnp.mean(centre * centre, axis=-1, keepdims=True))
    return centre * lax.rsqrt(spread + EPSILON) * gain

def to_half(values):
    return lax.optimization_barrier(values.astype(jnp.bfloat16))

def atom_window(queries, padded, biases, valid, heads):
    windows = queries.shape[0] // QWIN
    width = queries.shape[1]
    head_size = width // heads
    span_blocks = KWIN // QWIN
    blocks = padded.reshape(windows + span_blocks - 1, QWIN, 2 * width)
    gathered = jnp.concatenate([blocks[offset:offset + windows] for offset in range(span_blocks)], axis=1)
    query_heads = queries.astype(jnp.float32).reshape(windows, QWIN, heads, head_size)
    key_heads = gathered[:, :, :width].astype(jnp.float32).reshape(windows, KWIN, heads, head_size)
    value_heads = gathered[:, :, width:].astype(jnp.float32).reshape(windows, KWIN, heads, head_size)
    scores = jnp.einsum('wqhd,wkhd->wqhk', query_heads, key_heads) * head_size ** (-0.5)
    scores = scores + biases.astype(jnp.float32).reshape(windows, QWIN, heads, KWIN)
    scores = jnp.where(valid[:, None, None, :], scores, -1e+30)
    largest = lax.optimization_barrier(jnp.max(scores, axis=-1, keepdims=True))
    weights = jnp.exp(scores - largest)
    totals = lax.optimization_barrier(jnp.sum(weights, axis=-1))
    rounded = to_half(weights).astype(jnp.float32)
    mixed = jnp.einsum('wqhk,wkhd->wqhd', rounded, value_heads) / totals[..., None]
    return mixed.reshape(windows * QWIN, width).astype(jnp.bfloat16)

def reference(atoms, atom_bias, atom_token, token_atoms, token_single, key_value, pair, atom_gain, atom_qkv, atom_out_weight, agg_weight, token_gain, query_gate_weight, pair_weight, out_weight):
    groups = TOKENS // GROUP_TOKENS
    head_size = C_TOKEN // HEADS
    key_heads = key_value[0].astype(jnp.float32).reshape(KEYS, HEADS, head_size)
    value_heads = key_value[1].astype(jnp.float32).reshape(KEYS, HEADS, head_size)
    windows = GROUP_ATOMS // QWIN
    positions = jnp.arange(windows)[:, None] * QWIN - RIM + jnp.arange(KWIN)[None, :]
    valid = (positions >= 0) & (positions < GROUP_ATOMS)

    def one_group(inputs):
        group_atoms, group_bias, group_token, group_counts, group_single, group_pair = inputs
        normed = layer_norm(group_atoms.astype(jnp.float32), atom_gain).astype(jnp.bfloat16)
        projected = jnp.dot(normed, atom_qkv, preferred_element_type=jnp.float32).astype(jnp.bfloat16)
        padded = jnp.pad(projected[:, C_ATOM:], ((RIM, RIM), (0, 0)))
        mixed = atom_window(projected[:, :C_ATOM], padded, group_bias, valid, ATOM_HEADS)
        updated = (group_atoms.astype(jnp.float32) + jnp.dot(mixed, atom_out_weight, preferred_element_type=jnp.float32)).astype(jnp.bfloat16)
        lifted = to_half(jax.nn.relu(jnp.dot(updated, agg_weight, preferred_element_type=jnp.float32)))
        sums = jax.ops.segment_sum(lifted.astype(jnp.float32), group_token, num_segments=GROUP_TOKENS)
        acts = sums / group_counts.astype(jnp.float32)[:, None] + group_single.astype(jnp.float32)
        token_normed = layer_norm(acts, token_gain).astype(jnp.bfloat16)
        queries = to_half(jnp.dot(token_normed, query_gate_weight[0], preferred_element_type=jnp.float32))
        gates = jax.nn.sigmoid(jnp.dot(token_normed, query_gate_weight[1], preferred_element_type=jnp.float32))
        biases = to_half(jnp.einsum('qkc,ch->qhk', group_pair.astype(jnp.float32), pair_weight.astype(jnp.float32)))
        query_heads = queries.astype(jnp.float32).reshape(GROUP_TOKENS, HEADS, head_size)
        scores = jnp.einsum('qhd,khd->qhk', query_heads, key_heads) * head_size ** (-0.5) + biases.astype(jnp.float32)
        largest = lax.optimization_barrier(jnp.max(scores, axis=-1, keepdims=True))
        weights = jnp.exp(scores - largest)
        totals = lax.optimization_barrier(jnp.sum(weights, axis=-1))
        rounded = to_half(weights).astype(jnp.float32)
        token_mixed = jnp.einsum('qhk,khd->qhd', rounded, value_heads) / totals[..., None]
        gated = (gates * token_mixed.reshape(GROUP_TOKENS, C_TOKEN)).astype(jnp.bfloat16)
        token_out = (acts + jnp.dot(gated, out_weight, preferred_element_type=jnp.float32)).astype(jnp.bfloat16)
        return (updated, token_out)
    stacked = (atoms.reshape(groups, GROUP_ATOMS, C_ATOM), atom_bias.reshape(groups, GROUP_ATOMS, ATOM_HEADS, KWIN), atom_token.reshape(groups, GROUP_ATOMS), token_atoms.reshape(groups, GROUP_TOKENS), token_single.reshape(groups, GROUP_TOKENS, C_TOKEN), pair.reshape(groups, GROUP_TOKENS, KEYS, PAIR))
    atom_out, token_out = lax.map(one_group, stacked)
    return (atom_out.reshape(ATOMS, C_ATOM), token_out.reshape(TOKENS, C_TOKEN))
```

```python
import functools

import jax
import jax.numpy as jnp
from jax import lax
from jax.experimental import pallas as pl
from jax.experimental.pallas import tpu as pltpu
from jax.sharding import PartitionSpec as P

MESH = pl.DeviceIdType.MESH
F32 = jnp.float32
BF16 = jnp.bfloat16

ATOM_HEADS = 4
QWIN = 32
KWIN = 128
RIM = 48
ROWS = 1280
PADDED = ROWS + 2 * RIM
WIDTH = 128
TOK = 128
CH = 768
HEADS = 16
HEAD = 48
KEYS = 64
CHUNKS = 3
CHUNK = CH // CHUNKS
EPSILON = 1e-05
NT = (((1,), (1,)), ((), ()))


def mm(a, b):
    return jnp.dot(a, b, preferred_element_type=F32)


def mm_nt(a, b):
    return lax.dot_general(a, b, NT, preferred_element_type=F32)


def iota(shape, axis):
    return lax.broadcasted_iota(jnp.int32, shape, axis)


def layer_norm(values, gain):
    centre = values - jnp.mean(values, axis=-1, keepdims=True)
    spread = jnp.mean(centre * centre, axis=-1, keepdims=True)
    return centre * lax.rsqrt(spread + EPSILON) * gain


def kernel(
    comm,
    atoms_hbm,
    bias_hbm,
    slot_ref,
    count_ref,
    single_hbm,
    kv_ref,
    pair_hbm,
    atom_gain_ref,
    qkv_ref,
    atom_out_ref,
    agg_ref,
    token_gain_ref,
    qg_hbm,
    pair_weight_ref,
    out_hbm,
    atom_update_hbm,
    token_update_hbm,
    ap,
    bias,
    single,
    pair,
    qs,
    ks,
    vs,
    mx,
    up,
    oh,
    lf,
    own_sum,
    sb,
    rb,
    wq,
    wo,
    kv,
    raw,
    tb,
    kbd,
    vbd,
    mbd,
    acts,
    tu,
    local_sem,
    halo_send,
    halo_recv,
    w_send,
    w_recv,
    o_send,
    o_recv,
    k_send,
    k_recv,
    x_send,
    x_recv,
):
    if comm:
        tok = lax.axis_index("tok")
        me = lax.axis_index("atom")
    else:
        tok = jnp.int32(5)
        me = jnp.int32(7)
    core = lax.rem(tok, 2)
    row = lax.rem(lax.div(tok, 2), 4)
    hi = lax.div(tok, 8)
    lo = lax.rem(me, 2)
    left = lax.rem(me + 31, 32)
    right = lax.rem(me + 1, 32)
    twin = tok + 1 - 2 * core

    def place(flip, step, who):
        high = 1 - hi if flip else hi
        return (high * 4 + lax.rem(row + step + 4, 4)) * 2 + who

    def target(r):
        flip, step = divmod(r, 4)
        return (place(flip, step, core), me + 1 - 2 * lo if flip else me)

    def origin(r, who):
        flip, step = divmod(r, 4)
        return place(flip, -step, who)

    peers = [target(r) for r in range(1, 8)] + [(twin, me), (tok, left), (tok, right)]
    if comm:
        barrier = pltpu.get_barrier_semaphore()
        for peer in peers:
            pl.semaphore_signal(barrier, inc=1, device_id=peer, device_id_type=MESH)

    def local(i, src, dst):
        copy = pltpu.make_async_copy(src, dst, local_sem.at[i])
        copy.start()
        return copy

    def block(which):
        return pl.ds(pl.multiple_of(which * HEAD, 16), HEAD)

    atoms_in = local(0, atoms_hbm, ap.at[pl.ds(RIM, ROWS)])
    out_in = local(1, out_hbm, wo.at[block(tok)])
    bias_in = local(2, bias_hbm, bias)
    pair_in = local(3, pair_hbm, pair)
    single_in = local(4, single_hbm, single)

    qg_in = local(7, qg_hbm, wq.at[:, block(tok), :])
    kv[tok, 0:4, :] = kv_ref[0].astype(F32)
    kv[tok, 4:8, :] = kv_ref[1].astype(F32)

    def send(src, dst, ssem, rsem, device):
        return pltpu.make_async_remote_copy(
            src_ref=src, dst_ref=dst, send_sem=ssem, recv_sem=rsem,
            device_id=device, device_id_type=MESH,
        )

    def w_copy(which, i, device):
        ref = wq.at[:, block(which), :]
        return send(ref, ref, w_send.at[i], w_recv.at[i], device)

    def o_copy(which, i, device):
        ref = wo.at[block(which)]
        return send(ref, ref, o_send.at[i], o_recv.at[i], device)

    def k_copy(which, i, device):
        ref = kv.at[which]
        return send(ref, ref, k_send.at[i], k_recv.at[i], device)

    def halo_copy(side):
        if side == 0:
            src, dst, device = pl.ds(ROWS, RIM), pl.ds(0, RIM), (tok, right)
        else:
            src, dst, device = pl.ds(RIM, RIM), pl.ds(ROWS + RIM, RIM), (tok, left)
        return send(ap.at[src], ap.at[dst], halo_send.at[side], halo_recv.at[side], device)

    sends = []

    def go(copy):
        copy.start()
        sends.append(copy)

    atoms_in.wait()
    out_in.wait()
    qg_in.wait()
    if comm:
        pl.semaphore_wait(barrier, len(peers))
        for side in range(2):
            go(halo_copy(side))
        for r in range(1, 8):
            go(k_copy(tok, r, target(r)))
        for r in range(1, 8):
            go(w_copy(tok, r, target(r)))
        for r in range(1, 8):
            go(o_copy(tok, r, target(r)))
        go(k_copy(tok, 8, (twin, me)))
        go(w_copy(tok, 8, (twin, me)))
        go(o_copy(tok, 8, (twin, me)))

    def forward(copy, r):
        if comm:
            copy(origin(r, core), r, (twin, me)).wait_recv()
            go(copy(origin(r, core), 8 + r, (twin, me)))

    def arrive(copy, r):
        if comm:
            copy(origin(r, 1 - core), 8 + r, (twin, me)).wait_recv()

    def project(start, count, with_queries):
        values = ap[pl.ds(start, count), :].astype(F32)
        normed = layer_norm(values, atom_gain_ref[...]).astype(BF16)
        projected = mm(normed, qkv_ref[...]).astype(BF16)
        if with_queries:
            qs[pl.ds(start - RIM, count), :] = projected[:, :WIDTH]
        ks[pl.ds(start, count), :] = projected[:, WIDTH : 2 * WIDTH]
        vs[pl.ds(start, count), 0:WIDTH] = projected[:, 2 * WIDTH :]
        vs[pl.ds(start, count), WIDTH : 2 * WIDTH] = jnp.ones((count, WIDTH), BF16)

    for part in range(5):
        project(RIM + part * 256, 256, True)

    lane = iota((QWIN, WIDTH), 1)
    head_of_lane = lax.div(lane, 32)
    head_masks = [(head_of_lane == h).astype(F32).astype(BF16) for h in range(ATOM_HEADS)]
    mix_row = iota((KWIN, KWIN), 0)
    mix_col = iota((KWIN, KWIN), 1)
    source = lax.rem(mix_row, QWIN) * ATOM_HEADS + lax.div(mix_row, QWIN)
    reorder = (mix_col == source).astype(F32).astype(BF16)
    scale = 32 ** (-0.5)
    low_end = jnp.where(me == 0, RIM, 0)
    high_end = jnp.where(me == 31, ROWS + RIM, PADDED)

    def window(start, edge):
        queries = qs[pl.ds(start, QWIN), :]
        expanded = jnp.concatenate([queries * mask for mask in head_masks], axis=0)
        scores = mm_nt(expanded, ks[pl.ds(start, KWIN), :]) * scale
        scores += mm(reorder, bias[pl.ds(start * ATOM_HEADS, KWIN), :])
        if edge:
            place_of_key = start + mix_col
            inside = (place_of_key >= low_end) & (place_of_key < high_end)
            scores = jnp.where(inside, scores, -1e30)
        largest = jnp.max(scores, axis=1, keepdims=True)
        weights = jnp.exp(scores - largest).astype(BF16)
        both = mm(weights, vs[pl.ds(start, KWIN), :])
        rows = [both[h * QWIN : (h + 1) * QWIN] for h in range(ATOM_HEADS)]
        mixed, totals = rows[0][:, :WIDTH], rows[0][:, WIDTH:]
        for h in range(1, ATOM_HEADS):
            mixed = jnp.where(head_of_lane == h, rows[h][:, :WIDTH], mixed)
            totals = jnp.where(head_of_lane == h, rows[h][:, WIDTH:], totals)
        mx[pl.ds(start, QWIN), :] = (mixed / totals).astype(BF16)

    bias_in.wait()

    def interior(i, carry):
        for u in range(8):
            window(pl.multiple_of((8 * i + 2 + u) * QWIN, QWIN), False)
        return carry

    lax.fori_loop(0, 4, interior, 0)

    if comm:
        for side in range(2):
            halo_copy(side).wait_recv()
    project(0, RIM, False)
    project(ROWS + RIM, RIM, False)
    for w in (34, 35, 36, 37):
        window(w * QWIN, False)
    for w in (38, 39, 0, 1):
        window(w * QWIN, True)

    for part in range(5):
        span = pl.ds(part * 256, 256)
        values = ap[pl.ds(RIM + part * 256, 256), :].astype(F32)
        up[span, :] = (values + mm(mx[span, :], atom_out_ref[...])).astype(BF16)
    atoms_out = local(5, up, atom_update_hbm)

    tokens = iota((3 * TOK, WIDTH), 0) + (me - 1) * TOK
    for b in range(ROWS // WIDTH):
        named = slot_ref[b : b + 1, :]
        oh[:, b * WIDTH : (b + 1) * WIDTH] = (tokens == named).astype(F32).astype(BF16)

    def x_copy(side, c):
        device = (tok, left) if side == 0 else (tok, right)
        return send(
            sb.at[side, c], rb.at[side, c], x_send.at[side, c], x_recv.at[side, c], device
        )

    for c in range(CHUNKS):
        columns = slice(c * CHUNK, (c + 1) * CHUNK)
        for part in range(5):
            span = pl.ds(part * 256, 256)
            lf[span, :] = jnp.maximum(mm(up[span, :], agg_ref[:, columns]), 0.0).astype(BF16)
        lifted = lf[...]
        sb[0, c] = mm(oh[0:TOK, :], lifted).astype(BF16)
        sb[1, c] = mm(oh[2 * TOK : 3 * TOK, :], lifted).astype(BF16)
        if comm:
            go(x_copy(0, c))
            go(x_copy(1, c))
        own_sum[:, columns] = mm(oh[TOK : 2 * TOK, :], lifted)

    pair_in.wait()
    pair_weights = pair_weight_ref[...]

    def pair_bias(i, carry):
        for u in range(4):
            j = i * 8 + u * 2
            features = jnp.concatenate(
                [pair[j], pair[j + TOK // 2], pair[j + 1], pair[j + 1 + TOK // 2]], axis=0
            )
            both = mm_nt(pair_weights, features)
            start = pl.multiple_of(j * HEADS, 2 * HEADS)
            raw[pl.ds(start, HEADS), :] = both[:, :WIDTH]
            raw[pl.ds(start + HEADS, HEADS), :] = both[:, WIDTH:]
        return carry

    lax.fori_loop(0, 8, pair_bias, 0)
    half = TOK // 2
    first = iota((half, WIDTH), 1) < KEYS
    for g in range(HEADS // 2):
        even = raw[pl.ds(2 * g, half, stride=HEADS), :]
        odd = raw[pl.ds(2 * g + 1, half, stride=HEADS), :]
        columns = slice(g * WIDTH, (g + 1) * WIDTH)
        tb[0:half, columns] = jnp.where(first, even, pltpu.roll(odd, KEYS, 1)).astype(BF16)
        tb[half:TOK, columns] = jnp.where(first, pltpu.roll(even, KEYS, 1), odd).astype(BF16)

    for r in range(1, 8):
        forward(k_copy, r)
        forward(w_copy, r)
    for r in range(1, 8):
        forward(o_copy, r)

    for r in range(8):
        arrive(k_copy, r)
    half_ch = CH // 2
    span8 = 8 * KEYS
    member = lax.div(iota((span8, half_ch), 0), KEYS) == lax.div(iota((span8, half_ch), 1), HEAD)
    mbd[...] = member.astype(F32).astype(BF16)
    gathered = kv[...]
    keys = gathered[:, 0:4, :].reshape(KEYS, CH).astype(BF16)
    values = gathered[:, 4:8, :].reshape(KEYS, CH).astype(BF16)
    for g in range(2):
        columns = slice(g * half_ch, (g + 1) * half_ch)
        for h in range(8):
            span = slice(h * KEYS, (h + 1) * KEYS)
            kbd[g, span, :] = keys[:, columns] * mbd[span, :]
            vbd[g, span, :] = values[:, columns] * mbd[span, :]

    single_in.wait()
    if comm:
        for c in range(CHUNKS):
            for side in range(2):
                x_copy(side, c).wait_recv()
    counts = jnp.broadcast_to(count_ref[...].astype(F32), (TOK, TOK)).T
    inverse = 1.0 / counts
    for c in range(CHUNKS):
        columns = slice(c * CHUNK, (c + 1) * CHUNK)
        sums = own_sum[:, columns] + rb[0, c].astype(F32) + rb[1, c].astype(F32)
        per = jnp.concatenate([inverse, inverse], axis=1)
        acts[:, columns] = sums * per + single[:, columns].astype(F32)
    normed = layer_norm(acts[...], token_gain_ref[...]).astype(BF16)

    for r in range(8):
        arrive(w_copy, r)
    queries = mm_nt(normed, wq[0]).astype(BF16)
    gates = jax.nn.sigmoid(mm_nt(normed, wq[1]))

    token_scale = HEAD ** (-0.5)
    low = iota((TOK, WIDTH), 1) < KEYS
    gated = []
    for g in range(2):
        columns = slice(g * half_ch, (g + 1) * half_ch)
        scores = mm_nt(queries[:, columns], kbd[g]) * token_scale
        scores += tb[:, g * span8 : (g + 1) * span8].astype(F32)
        weights = []
        for i in range(4):
            part = scores[:, i * WIDTH : (i + 1) * WIDTH]
            top_low = jnp.max(jnp.where(low, part, -jnp.inf), axis=1, keepdims=True)
            top_high = jnp.max(jnp.where(low, -jnp.inf, part), axis=1, keepdims=True)
            weights.append(jnp.exp(part - jnp.where(low, top_low, top_high)).astype(BF16))
        weights = jnp.concatenate(weights, axis=1)
        mixed = mm(weights, vbd[g]) / mm(weights, mbd[...])
        gated.append((gates[:, columns] * mixed).astype(BF16))
    gated = jnp.concatenate(gated, axis=1)

    for r in range(8):
        arrive(o_copy, r)
    tu[...] = (acts[...] + mm(gated, wo[...])).astype(BF16)
    tokens_out = local(6, tu, token_update_hbm)
    for copy in sends:
        copy.wait_send()
    atoms_out.wait()
    tokens_out.wait()


def call(comm, *args):
    hbm = pl.BlockSpec(memory_space=pl.ANY)
    vmem = pl.BlockSpec(memory_space=pltpu.VMEM)
    v = pltpu.VMEM
    dma = pltpu.SemaphoreType.DMA
    return pl.pallas_call(
        functools.partial(kernel, comm),
        out_shape=(
            jax.ShapeDtypeStruct((ROWS, WIDTH), BF16),
            jax.ShapeDtypeStruct((TOK, CH), BF16),
        ),
        in_specs=[hbm, hbm, vmem, vmem, hbm, vmem, hbm] + [vmem] * 5 + [hbm, vmem, hbm],
        out_specs=(hbm, hbm),
        scratch_shapes=[
            v((PADDED, WIDTH), BF16),
            v((ROWS * ATOM_HEADS, KWIN), BF16),
            v((TOK, CH), BF16),
            v((TOK, KEYS, WIDTH), BF16),
            v((ROWS, WIDTH), BF16),
            v((PADDED, WIDTH), BF16),
            v((PADDED, 2 * WIDTH), BF16),
            v((ROWS, WIDTH), BF16),
            v((ROWS, WIDTH), BF16),
            v((3 * TOK, ROWS), BF16),
            v((ROWS, CHUNK), BF16),
            v((TOK, CH), F32),
            v((2, CHUNKS, TOK, CHUNK), BF16),
            v((2, CHUNKS, TOK, CHUNK), BF16),
            v((2, CH, CH), BF16),
            v((CH, CH), BF16),
            v((HEADS, 8, CH), F32),
            v((TOK // 2 * HEADS, WIDTH), F32),
            v((TOK, HEADS * KEYS), BF16),
            v((2, 8 * KEYS, CH // 2), BF16),
            v((2, 8 * KEYS, CH // 2), BF16),
            v((8 * KEYS, CH // 2), BF16),
            v((TOK, CH), F32),
            v((TOK, CH), BF16),
            dma((8,)),
            dma((2,)),
            dma((2,)),
            dma((16,)),
            dma((16,)),
            dma((16,)),
            dma((16,)),
            dma((16,)),
            dma((16,)),
            dma((2, CHUNKS)),
            dma((2, CHUNKS)),
        ],
        compiler_params=pltpu.CompilerParams(
            collective_id=0 if comm else None,
            has_side_effects=True,
            vmem_limit_bytes=60 * 1024 * 1024,
        ),
    )(*args)


def body(
    atoms,
    atom_bias,
    atom_token,
    token_atoms,
    token_single,
    key_value,
    pair,
    atom_gain,
    atom_qkv,
    atom_out_weight,
    agg_weight,
    token_gain,
    query_gate_weight,
    pair_weight,
    out_weight,
    comm=True,
):
    return call(
        comm,
        atoms,
        atom_bias.reshape(ROWS * ATOM_HEADS, KWIN),
        atom_token.reshape(ROWS // WIDTH, WIDTH),
        token_atoms.reshape(1, TOK),
        token_single,
        key_value,
        pair,
        atom_gain.reshape(1, WIDTH),
        atom_qkv,
        atom_out_weight,
        agg_weight,
        token_gain.reshape(1, CH),
        query_gate_weight.transpose(0, 2, 1),
        pair_weight.T,
        out_weight,
    )


def solution(mesh):
    return jax.shard_map(
        body,
        mesh=mesh,
        in_specs=(
            P(("tok", "atom"), None),
            P(("tok", "atom"), None, None),
            P(("tok", "atom")),
            P(("tok", "atom")),
            P(("tok", "atom"), None),
            P(None, "tok", None),
            P(("tok", "atom"), None, None),
            P(),
            P(),
            P(),
            P(),
            P(),
            P(None, None, "tok"),
            P(),
            P("tok", None),
        ),
        out_specs=(P(("tok", "atom"), None), P(("tok", "atom"), None)),
        check_vma=False,
    )
```

```python
import functools

import jax
import jax.numpy as jnp
from jax import lax
from jax.experimental import pallas as pl
from jax.experimental.pallas import tpu as pltpu
from jax.sharding import PartitionSpec as P

MESH = pl.DeviceIdType.MESH
F32 = jnp.float32
BF16 = jnp.bfloat16

ATOM_HEADS = 4
QWIN = 32
KWIN = 128
RIM = 48
ROWS = 1280
PADDED = ROWS + 2 * RIM
WINDOWS = ROWS // QWIN
WIDTH = 128
TOK = 128
CH = 768
HEADS = 16
HEAD = 48
HALF = CH // 2
KEYS = 64
CHUNKS = 3
CHUNK = CH // CHUNKS
EPSILON = 1e-05
PIECES = ((0, 0), (0, 1), (0, -1), (1, 0), (0, 2), (1, 1), (1, -1), (1, 2))
NT = (((1,), (1,)), ((), ()))


def mm(a, b):
    return jnp.dot(a, b, preferred_element_type=F32)


def mm_nt(a, b):
    return lax.dot_general(a, b, NT, preferred_element_type=F32)


def iota(shape, axis):
    return lax.broadcasted_iota(jnp.int32, shape, axis)


def layer_norm(values, gain):
    centre = values - jnp.mean(values, axis=-1, keepdims=True)
    spread = jnp.mean(centre * centre, axis=-1, keepdims=True)
    return centre * lax.rsqrt(spread + EPSILON) * gain


def kernel(
    comm,
    atoms_hbm,
    bias_hbm,
    slot_hbm,
    count_hbm,
    single_hbm,
    kv_hbm,
    pair_hbm,
    atom_gain_hbm,
    qkv_hbm,
    atom_out_hbm,
    agg_hbm,
    token_gain_hbm,
    qg_hbm,
    pair_weight_hbm,
    out_hbm,
    up,
    tu,
    ap,
    bias,
    single,
    pair,
    qs,
    ks,
    kt,
    vs,
    mx,
    oh,
    lf,
    own_sum,
    sb,
    rb,
    wq,
    wo,
    kv,
    raw,
    tb,
    kbd,
    vbd,
    mbd,
    acts,
    slot_ref,
    count_ref,
    kv_ref,
    atom_gain_ref,
    qkv_ref,
    atom_out_ref,
    agg_ref,
    token_gain_ref,
    pair_weight_ref,
    local_sem,
    send_sem,
    halo_recv,
    w_recv,
    d_recv,
    o_recv,
    k_recv,
    wt_recv,
    ot_recv,
    kt_recv,
    x_recv,
):
    if comm:
        tok = lax.axis_index("tok")
        me = lax.axis_index("atom")
    else:
        tok = jnp.int32(5)
        me = jnp.int32(7)
    core = lax.rem(tok, 2)
    row = lax.rem(lax.div(tok, 2), 4)
    hi = lax.div(tok, 8)
    lo = lax.rem(me, 2)
    left = lax.rem(me + 31, 32)
    right = lax.rem(me + 1, 32)
    twin = tok + 1 - 2 * core

    def place(flip, step, who):
        high = 1 - hi if flip else hi
        return (high * 4 + lax.rem(row + step + 4, 4)) * 2 + who

    def origin(piece, who):
        flip, step = PIECES[piece]
        return place(flip, step, who)

    across = me + 1 - 2 * lo
    up_device = (place(0, 1, core), me)
    down_device = (place(0, -1, core), me)
    across_device = (place(1, 0, core), across)
    twin_device = (twin, me)
    left_device = (tok, left)
    right_device = (tok, right)
    targets = [(place(flip, -step, core), across if flip else me) for flip, step in PIECES]
    peers = targets[1:] + [twin_device, left_device, right_device]
    if comm:
        barrier = pltpu.get_barrier_semaphore()
        for peer in peers:
            pl.semaphore_signal(barrier, inc=1, device_id=peer, device_id_type=MESH)

    def local(i, src, dst):
        copy = pltpu.make_async_copy(src, dst, local_sem.at[i])
        copy.start()
        return copy

    def block(which):
        return pl.ds(pl.multiple_of(which * HEAD, 16), HEAD)

    qg_in = local(7, qg_hbm, wq.at[:, block(tok), :])
    out_in = local(1, out_hbm, wo.at[block(tok)])
    kv_in = local(8, kv_hbm, kv_ref)
    atoms_in = local(0, atoms_hbm, ap.at[pl.ds(RIM, ROWS)])
    gain_in = local(9, atom_gain_hbm, atom_gain_ref)
    qkv_in = local(10, qkv_hbm, qkv_ref)
    bias_in = local(2, bias_hbm, bias)
    small_in = [
        local(11, atom_out_hbm, atom_out_ref),
        local(12, agg_hbm, agg_ref),
        local(13, slot_hbm, slot_ref),
        local(14, count_hbm, count_ref),
        local(15, token_gain_hbm, token_gain_ref),
        local(16, pair_weight_hbm, pair_weight_ref),
    ]
    pair_in = local(3, pair_hbm, pair)
    single_in = local(4, single_hbm, single)

    started = []

    def send(src, dst, recv, device):
        return pltpu.make_async_remote_copy(
            src_ref=src, dst_ref=dst, send_sem=send_sem.at[len(started)], recv_sem=recv,
            device_id=device, device_id_type=MESH,
        )

    def go(ref, recv, device, target=None):
        if comm:
            copy = send(ref, ref if target is None else target, recv, device)
            copy.start()
            started.append(copy)

    def await_copy(ref, recv):
        if comm:
            send(ref, ref, recv, twin_device).wait_recv()

    def w_ref(piece, who):
        return wq.at[:, block(origin(piece, who)), :]

    def half_ref(piece, m):
        return wq.at[m, block(origin(piece, core)), :]

    def o_ref(piece, who):
        return wo.at[block(origin(piece, who))]

    def k_ref(piece, who):
        return kv.at[origin(piece, who)]

    def to_twin(ref_of, twin_recv, piece):
        go(ref_of(piece, core), twin_recv.at[piece], twin_device)

    def relay_first():
        for piece in (1, 2, 3):
            await_copy(w_ref(piece, core), w_recv.at[piece])
        go(half_ref(1, 0), d_recv.at[0], down_device)
        go(half_ref(2, 1), d_recv.at[1], up_device)
        go(w_ref(3, core), w_recv.at[6], up_device)
        go(w_ref(3, core), w_recv.at[5], down_device)
        for device, piece in ((up_device, 2), (down_device, 1), (across_device, 3)):
            go(o_ref(0, core), o_recv.at[piece], device)
        for piece in (1, 2, 3):
            to_twin(w_ref, wt_recv, piece)

    def relay_second():
        await_copy(half_ref(4, 0), d_recv.at[0])
        await_copy(half_ref(4, 1), d_recv.at[1])
        go(w_ref(4, core), w_recv.at[7], across_device)
        for piece in (1, 2, 3):
            await_copy(o_ref(piece, core), o_recv.at[piece])
        go(o_ref(1, core), o_recv.at[4], down_device)
        go(o_ref(3, core), o_recv.at[6], up_device)
        go(o_ref(3, core), o_recv.at[5], down_device)
        to_twin(w_ref, wt_recv, 4)
        for piece in (1, 2, 3):
            to_twin(o_ref, ot_recv, piece)
        for piece in range(1, 8):
            await_copy(k_ref(piece, core), k_recv.at[piece])
            to_twin(k_ref, kt_recv, piece)

    def relay_third():
        await_copy(o_ref(4, core), o_recv.at[4])
        go(o_ref(4, core), o_recv.at[7], across_device)
        for piece in (5, 6, 7):
            await_copy(w_ref(piece, core), w_recv.at[piece])
            to_twin(w_ref, wt_recv, piece)
        to_twin(o_ref, ot_recv, 4)

    def relay_fourth():
        for piece in (5, 6, 7):
            await_copy(o_ref(piece, core), o_recv.at[piece])
            to_twin(o_ref, ot_recv, piece)

    def arrive(ref_of, twin_recv):
        for piece in range(8):
            await_copy(ref_of(piece, 1 - core), twin_recv.at[piece])

    kv_in.wait()
    both = kv_ref[...].astype(F32)
    kv[tok] = jnp.concatenate(
        [both[0, :, :HALF], both[1, :, :HALF], both[0, :, HALF:], both[1, :, HALF:]], axis=0
    ).astype(BF16)
    qg_in.wait()
    atoms_in.wait()
    out_in.wait()
    if comm:
        pl.semaphore_wait(barrier, len(peers))
    for device, piece in ((up_device, 2), (down_device, 1), (across_device, 3)):
        go(w_ref(0, core), w_recv.at[piece], device)
    last, first = pl.ds(ROWS, RIM), pl.ds(RIM, RIM)
    low, high = pl.ds(0, RIM), pl.ds(ROWS + RIM, RIM)
    go(ap.at[last], halo_recv.at[0], right_device, ap.at[low])
    go(ap.at[first], halo_recv.at[1], left_device, ap.at[high])
    for piece in range(1, 8):
        go(k_ref(0, core), k_recv.at[piece], targets[piece])
    to_twin(w_ref, wt_recv, 0)
    to_twin(o_ref, ot_recv, 0)
    to_twin(k_ref, kt_recv, 0)

    def project(start, count, with_queries):
        values = ap[pl.ds(start, count), :].astype(F32)
        normed = layer_norm(values, atom_gain_ref[...]).astype(BF16)
        projected = mm(normed, qkv_ref[...]).astype(BF16)
        if with_queries:
            qs[pl.ds(start - RIM, count), :] = projected[:, :WIDTH]
        ks[pl.ds(start, count), :] = projected[:, WIDTH : 2 * WIDTH]
        vs[pl.ds(start, count), 0:WIDTH] = projected[:, 2 * WIDTH :]
        vs[pl.ds(start, count), WIDTH : 2 * WIDTH] = jnp.ones((count, WIDTH), BF16)

    gain_in.wait()
    qkv_in.wait()
    for part in range(5):
        project(RIM + part * 256, 256, True)

    lane = iota((QWIN, WIDTH), 1)
    head_of_lane = lax.div(lane, 32)
    head_masks = [(head_of_lane == h).astype(F32).astype(BF16) for h in range(ATOM_HEADS)]
    mix_row = iota((KWIN, KWIN), 0)
    mix_col = iota((KWIN, KWIN), 1)
    source = lax.rem(mix_row, QWIN) * ATOM_HEADS + lax.div(mix_row, QWIN)
    reorder = (mix_col == source).astype(F32).astype(BF16)
    scale = 32 ** (-0.5)
    low_end = jnp.where(me == 0, RIM, 0)
    high_end = jnp.where(me == 31, ROWS + RIM, PADDED)

    def window(w, edge):
        start = pl.multiple_of(w * QWIN, QWIN)
        queries = qs[pl.ds(start, QWIN), :]
        expanded = jnp.concatenate([queries * mask for mask in head_masks], axis=0)
        scores = mm(expanded, kt[w]) * scale
        scores += mm(reorder, bias[pl.ds(start * ATOM_HEADS, KWIN), :])
        if edge:
            place_of_key = start + mix_col
            inside = (place_of_key >= low_end) & (place_of_key < high_end)
            scores = jnp.where(inside, scores, -1e30)
        largest = jnp.max(scores, axis=1, keepdims=True)
        weights = jnp.exp(scores - largest).astype(BF16)
        both = mm(weights, vs[pl.ds(start, KWIN), :])
        rows = [both[h * QWIN : (h + 1) * QWIN] for h in range(ATOM_HEADS)]
        mixed, totals = rows[0][:, :WIDTH], rows[0][:, WIDTH:]
        for h in range(1, ATOM_HEADS):
            mixed = jnp.where(head_of_lane == h, rows[h][:, :WIDTH], mixed)
            totals = jnp.where(head_of_lane == h, rows[h][:, WIDTH:], totals)
        mx[pl.ds(start, QWIN), :] = (mixed / totals).astype(BF16)

    def transposed_keys(w):
        kt[w] = ks[pl.ds(pl.multiple_of(w * QWIN, QWIN), KWIN), :].T

    def turn(i, carry):
        for u in range(6):
            transposed_keys(6 * i + 2 + u)
        return carry

    lax.fori_loop(0, 6, turn, 0)
    bias_in.wait()

    def interior(i, carry):
        for u in range(8):
            window(8 * i + 2 + u, False)
        return carry

    lax.fori_loop(0, 4, interior, 0)

    relay_first()
    await_copy(ap.at[low], halo_recv.at[0])
    await_copy(ap.at[high], halo_recv.at[1])
    project(0, RIM, False)
    project(ROWS + RIM, RIM, False)
    for w in (38, 39, 0, 1):
        transposed_keys(w)
    for w in (34, 35, 36, 37):
        window(w, False)
    for w in (38, 39, 0, 1):
        window(w, True)

    for copy in small_in:
        copy.wait()
    for part in range(5):
        span = pl.ds(part * 256, 256)
        values = ap[pl.ds(RIM + part * 256, 256), :].astype(F32)
        up[span, :] = (values + mm(mx[span, :], atom_out_ref[...])).astype(BF16)

    tokens = iota((3 * TOK, WIDTH), 0) + (me - 1) * TOK
    for b in range(ROWS // WIDTH):
        named = slot_ref[b : b + 1, :]
        oh[:, b * WIDTH : (b + 1) * WIDTH] = (tokens == named).astype(F32).astype(BF16)

    for c in range(CHUNKS):
        columns = slice(c * CHUNK, (c + 1) * CHUNK)
        for part in range(5):
            span = pl.ds(part * 256, 256)
            lf[span, :] = jnp.maximum(mm(up[span, :], agg_ref[:, columns]), 0.0).astype(BF16)
        lifted = lf[...]
        sb[0, c] = mm(oh[0:TOK, :], lifted).astype(BF16)
        sb[1, c] = mm(oh[2 * TOK : 3 * TOK, :], lifted).astype(BF16)
        go(sb.at[0, c], x_recv.at[0, c], left_device, rb.at[0, c])
        go(sb.at[1, c], x_recv.at[1, c], right_device, rb.at[1, c])
        own_sum[:, columns] = mm(oh[TOK : 2 * TOK, :], lifted)

    relay_second()
    pair_in.wait()
    pair_weights = pair_weight_ref[...]

    def pair_bias(i, carry):
        for u in range(4):
            j = i * 8 + u * 2
            features = jnp.concatenate(
                [pair[j], pair[j + TOK // 2], pair[j + 1], pair[j + 1 + TOK // 2]], axis=0
            )
            both = mm_nt(pair_weights, features)
            start = pl.multiple_of(j * HEADS, 2 * HEADS)
            raw[pl.ds(start, HEADS), :] = both[:, :WIDTH]
            raw[pl.ds(start + HEADS, HEADS), :] = both[:, WIDTH:]
        return carry

    lax.fori_loop(0, 8, pair_bias, 0)
    relay_third()
    half = TOK // 2
    first_key = iota((half, WIDTH), 1) < KEYS
    for g in range(HEADS // 2):
        even = raw[pl.ds(2 * g, half, stride=HEADS), :]
        odd = raw[pl.ds(2 * g + 1, half, stride=HEADS), :]
        columns = slice(g * WIDTH, (g + 1) * WIDTH)
        tb[0:half, columns] = jnp.where(first_key, even, pltpu.roll(odd, KEYS, 1)).astype(BF16)
        tb[half:TOK, columns] = jnp.where(first_key, pltpu.roll(even, KEYS, 1), odd).astype(BF16)

    arrive(k_ref, kt_recv)
    span8 = 8 * KEYS
    member = lax.div(iota((span8, HALF), 0), KEYS) == lax.div(iota((span8, HALF), 1), HEAD)
    mbd[...] = member.astype(F32).astype(BF16)
    gathered = kv[...].astype(F32)
    for g in range(2):
        keys = gathered[:, 8 * g : 8 * g + 4, :].reshape(KEYS, HALF).astype(BF16)
        values = gathered[:, 8 * g + 4 : 8 * g + 8, :].reshape(KEYS, HALF).astype(BF16)
        for h in range(8):
            span = slice(h * KEYS, (h + 1) * KEYS)
            kbd[g, span, :] = keys * mbd[span, :]
            vbd[g, span, :] = values * mbd[span, :]

    relay_fourth()
    single_in.wait()
    for c in range(CHUNKS):
        for side in range(2):
            await_copy(rb.at[side, c], x_recv.at[side, c])
    counts = jnp.broadcast_to(count_ref[...].astype(F32), (TOK, TOK)).T
    inverse = 1.0 / counts
    for c in range(CHUNKS):
        columns = slice(c * CHUNK, (c + 1) * CHUNK)
        sums = own_sum[:, columns] + rb[0, c].astype(F32) + rb[1, c].astype(F32)
        per = jnp.concatenate([inverse, inverse], axis=1)
        acts[:, columns] = sums * per + single[:, columns].astype(F32)
    gain = jnp.concatenate([token_gain_ref[i : i + 1, :] for i in range(CH // WIDTH)], axis=1)
    normed = layer_norm(acts[...], gain).astype(BF16)

    arrive(w_ref, wt_recv)
    queries = mm_nt(normed, wq[0]).astype(BF16)
    gates = jax.nn.sigmoid(mm_nt(normed, wq[1]))

    token_scale = HEAD ** (-0.5)
    low = iota((TOK, WIDTH), 1) < KEYS
    gated = []
    for g in range(2):
        columns = slice(g * HALF, (g + 1) * HALF)
        scores = mm_nt(queries[:, columns], kbd[g]) * token_scale
        scores += tb[:, g * span8 : (g + 1) * span8].astype(F32)
        weights = []
        for i in range(4):
            part = scores[:, i * WIDTH : (i + 1) * WIDTH]
            top_low = jnp.max(jnp.where(low, part, -jnp.inf), axis=1, keepdims=True)
            top_high = jnp.max(jnp.where(low, -jnp.inf, part), axis=1, keepdims=True)
            weights.append(jnp.exp(part - jnp.where(low, top_low, top_high)).astype(BF16))
        weights = jnp.concatenate(weights, axis=1)
        mixed = mm(weights, vbd[g]) / mm(weights, mbd[...])
        gated.append((gates[:, columns] * mixed).astype(BF16))
    gated = jnp.concatenate(gated, axis=1)

    arrive(o_ref, ot_recv)
    tu[...] = (acts[...] + mm(gated, wo[...])).astype(BF16)
    for copy in started:
        copy.wait_send()


def call(comm, *args):
    hbm = pl.BlockSpec(memory_space=pl.ANY)
    v = pltpu.VMEM
    dma = pltpu.SemaphoreType.DMA
    return pl.pallas_call(
        functools.partial(kernel, comm),
        out_shape=(v((ROWS, WIDTH), BF16), v((TOK, CH), BF16)),
        in_specs=[hbm] * 15,
        out_specs=(pl.BlockSpec(memory_space=v), pl.BlockSpec(memory_space=v)),
        scratch_shapes=[
            v((PADDED, WIDTH), BF16),
            v((ROWS * ATOM_HEADS, KWIN), BF16),
            v((TOK, CH), BF16),
            v((TOK, KEYS, WIDTH), BF16),
            v((ROWS, WIDTH), BF16),
            v((PADDED, WIDTH), BF16),
            v((WINDOWS, WIDTH, KWIN), BF16),
            v((PADDED, 2 * WIDTH), BF16),
            v((ROWS, WIDTH), BF16),
            v((3 * TOK, ROWS), BF16),
            v((ROWS, CHUNK), BF16),
            v((TOK, CH), F32),
            v((2, CHUNKS, TOK, CHUNK), BF16),
            v((2, CHUNKS, TOK, CHUNK), BF16),
            v((2, CH, CH), BF16),
            v((CH, CH), BF16),
            v((HEADS, 16, CH // 2), BF16),
            v((TOK // 2 * HEADS, WIDTH), F32),
            v((TOK, HEADS * KEYS), BF16),
            v((2, 8 * KEYS, CH // 2), BF16),
            v((2, 8 * KEYS, CH // 2), BF16),
            v((8 * KEYS, CH // 2), BF16),
            v((TOK, CH), F32),
            v((ROWS // WIDTH, WIDTH), jnp.int32),
            v((1, TOK), jnp.int32),
            v((2, 4, CH), BF16),
            v((1, WIDTH), F32),
            v((WIDTH, 3 * WIDTH), BF16),
            v((WIDTH, WIDTH), BF16),
            v((WIDTH, CH), BF16),
            v((CH // WIDTH, WIDTH), F32),
            v((HEADS, WIDTH), BF16),
            dma((17,)),
            dma((72,)),
            dma((2,)),
            dma((8,)),
            dma((2,)),
            dma((8,)),
            dma((8,)),
            dma((8,)),
            dma((8,)),
            dma((8,)),
            dma((2, CHUNKS)),
        ],
        compiler_params=pltpu.CompilerParams(
            collective_id=0 if comm else None,
            has_side_effects=True,
            vmem_limit_bytes=60 * 1024 * 1024,
        ),
    )(*args)


def write_kernel(up, tu, atom_update, token_update, sems):
    copies = [
        pltpu.make_async_copy(up, atom_update, sems.at[0]),
        pltpu.make_async_copy(tu, token_update, sems.at[1]),
    ]
    for copy in copies:
        copy.start()
    for copy in copies:
        copy.wait()


def write(up, tu):
    hbm = pl.BlockSpec(memory_space=pl.ANY)
    return pl.pallas_call(
        write_kernel,
        out_shape=(
            jax.ShapeDtypeStruct((ROWS, WIDTH), BF16),
            jax.ShapeDtypeStruct((TOK, CH), BF16),
        ),
        in_specs=[pl.BlockSpec(memory_space=pltpu.VMEM)] * 2,
        out_specs=(hbm, hbm),
        scratch_shapes=[pltpu.SemaphoreType.DMA((2,))],
        compiler_params=pltpu.CompilerParams(vmem_limit_bytes=8 * 1024 * 1024),
    )(up, tu)


def body(
    atoms,
    atom_bias,
    atom_token,
    token_atoms,
    token_single,
    key_value,
    pair,
    atom_gain,
    atom_qkv,
    atom_out_weight,
    agg_weight,
    token_gain,
    query_gate_weight,
    pair_weight,
    out_weight,
    comm=True,
):
    up, tu = call(
        comm,
        atoms,
        atom_bias.reshape(ROWS * ATOM_HEADS, KWIN),
        atom_token.reshape(ROWS // WIDTH, WIDTH),
        token_atoms.reshape(1, TOK),
        token_single,
        key_value,
        pair,
        atom_gain.reshape(1, WIDTH),
        atom_qkv,
        atom_out_weight,
        agg_weight,
        token_gain.reshape(CH // WIDTH, WIDTH),
        query_gate_weight.transpose(0, 2, 1),
        pair_weight.T,
        out_weight,
    )
    return write(up, tu)


def solution(mesh):
    return jax.shard_map(
        body,
        mesh=mesh,
        in_specs=(
            P(("tok", "atom"), None),
            P(("tok", "atom"), None, None),
            P(("tok", "atom")),
            P(("tok", "atom")),
            P(("tok", "atom"), None),
            P(None, "tok", None),
            P(("tok", "atom"), None, None),
            P(),
            P(),
            P(),
            P(),
            P(),
            P(None, None, "tok"),
            P(),
            P("tok", None),
        ),
        out_specs=(P(("tok", "atom"), None), P(("tok", "atom"), None)),
        check_vma=False,
    )
```

```python
import functools

import jax
import jax.numpy as jnp
from jax import lax
from jax.experimental import pallas as pl
from jax.experimental.pallas import tpu as pltpu
from jax.sharding import PartitionSpec as P

MESH = pl.DeviceIdType.MESH
F32 = jnp.float32
BF16 = jnp.bfloat16

ATOM_HEADS = 4
QWIN = 32
KWIN = 128
RIM = 48
ROWS = 1280
PADDED = ROWS + 2 * RIM
WINDOWS = ROWS // QWIN
WIDTH = 128
TOK = 128
CH = 768
HEADS = 16
HEAD = 48
HALF = CH // 2
KEYS = 64
CHUNKS = 3
CHUNK = CH // CHUNKS
EPSILON = 1e-05
PIECES = ((0, 0), (0, 1), (0, -1), (1, 0), (0, 2), (1, 1), (1, -1), (1, 2))
OWN, AHEAD, BEHIND, ACROSS, FAR, NEAR_ACROSS, OTHER_ACROSS, FAR_ACROSS = range(8)
NT = (((1,), (1,)), ((), ()))


def mm(a, b):
    return jnp.dot(a, b, preferred_element_type=F32)


def mm_nt(a, b):
    return lax.dot_general(a, b, NT, preferred_element_type=F32)


def iota(shape, axis):
    return lax.broadcasted_iota(jnp.int32, shape, axis)


def layer_norm(values, gain):
    centre = values - jnp.mean(values, axis=-1, keepdims=True)
    spread = jnp.mean(centre * centre, axis=-1, keepdims=True)
    return centre * lax.rsqrt(spread + EPSILON) * gain


def kernel(
    comm,
    atoms_hbm,
    bias_hbm,
    slot_hbm,
    count_hbm,
    single_hbm,
    kv_hbm,
    pair_hbm,
    atom_gain_hbm,
    qkv_hbm,
    atom_out_hbm,
    agg_hbm,
    token_gain_hbm,
    qg_hbm,
    pair_weight_hbm,
    out_hbm,
    up,
    tu,
    ap,
    bias,
    single,
    pair,
    qs,
    ks,
    kt,
    vs,
    mx,
    oh,
    lf,
    own_sum,
    sb,
    rb,
    wq,
    wo,
    kv,
    raw,
    tb,
    kbd,
    vbd,
    mbd,
    acts,
    slot_ref,
    count_ref,
    kv_ref,
    atom_gain_ref,
    qkv_ref,
    atom_out_ref,
    agg_ref,
    token_gain_ref,
    pair_weight_ref,
    local_sem,
    send_sem,
    halo_recv,
    u_recv,
    twin_recv,
    k_recv,
    kt_recv,
    x_recv,
):
    if comm:
        tok = lax.axis_index("tok")
        me = lax.axis_index("atom")
    else:
        tok = jnp.int32(5)
        me = jnp.int32(7)
    core = lax.rem(tok, 2)
    row = lax.rem(lax.div(tok, 2), 4)
    hi = lax.div(tok, 8)
    lo = lax.rem(me, 2)
    left = lax.rem(me + 31, 32)
    right = lax.rem(me + 1, 32)
    twin = tok + 1 - 2 * core

    def place(flip, step, who):
        high = 1 - hi if flip else hi
        return (high * 4 + lax.rem(row + step + 4, 4)) * 2 + who

    sign = 1 - 2 * lax.rem(lax.div(me, 2), 2)

    def origin(piece, who):
        flip, step = PIECES[piece]
        return place(flip, step if piece < FAR else sign * step, who)

    across = me + 1 - 2 * lo
    up_device = (place(0, 1, core), me)
    down_device = (place(0, -1, core), me)
    across_device = (place(1, 0, core), across)
    twin_device = (twin, me)
    left_device = (tok, left)
    right_device = (tok, right)
    sign_device = (place(0, sign, core), me)
    back_device = (place(0, -sign, core), me)
    above_device = (tok, lax.rem(me + 2, 32))
    below_device = (tok, lax.rem(me + 30, 32))
    targets = []
    for piece, (flip, step) in enumerate(PIECES):
        steps = -step if piece < FAR else -sign * step
        targets.append((place(flip, steps, core), across if flip else me))
    peers = targets[1:] + [twin_device, left_device, right_device, above_device, below_device]
    if comm:
        barrier = pltpu.get_barrier_semaphore()
        for peer in peers:
            pl.semaphore_signal(barrier, inc=1, device_id=peer, device_id_type=MESH)

    def local(i, src, dst):
        copy = pltpu.make_async_copy(src, dst, local_sem.at[i])
        copy.start()
        return copy

    def block(which):
        return pl.ds(pl.multiple_of(which * HEAD, 16), HEAD)

    qg_in = local(7, qg_hbm, wq.at[:, block(tok), :])
    out_in = local(1, out_hbm, wo.at[block(tok)])
    kv_in = local(8, kv_hbm, kv_ref)
    atoms_in = local(0, atoms_hbm, ap.at[pl.ds(RIM, ROWS)])
    gain_in = local(9, atom_gain_hbm, atom_gain_ref)
    qkv_in = local(10, qkv_hbm, qkv_ref)
    slot_in = local(13, slot_hbm, slot_ref)
    bias_in = local(2, bias_hbm, bias)
    small_in = [
        local(11, atom_out_hbm, atom_out_ref),
        local(12, agg_hbm, agg_ref),
        local(14, count_hbm, count_ref),
        local(15, token_gain_hbm, token_gain_ref),
        local(16, pair_weight_hbm, pair_weight_ref),
    ]
    pair_in = local(3, pair_hbm, pair)
    single_in = local(4, single_hbm, single)

    started = []

    def send(src, dst, recv, device):
        return pltpu.make_async_remote_copy(
            src_ref=src, dst_ref=dst, send_sem=send_sem.at[len(started)], recv_sem=recv,
            device_id=device, device_id_type=MESH,
        )

    def go(ref, recv, device, target=None):
        if comm:
            copy = send(ref, ref if target is None else target, recv, device)
            copy.start()
            started.append(copy)

    def await_copy(ref, recv):
        if comm:
            send(ref, ref, recv, twin_device).wait_recv()

    def unit_ref(tok_of, unit):
        return wq.at[unit, block(tok_of), :] if unit < 2 else wo.at[block(tok_of)]

    def k_ref(piece, who):
        return kv.at[origin(piece, who)]

    def pass_on(piece, unit, name, device):
        go(unit_ref(origin(piece, core), unit), u_recv.at[name, unit], device)

    def direct(unit):
        pass_on(OWN, unit, BEHIND, up_device)
        pass_on(OWN, unit, AHEAD, down_device)
        pass_on(OWN, unit, ACROSS, across_device)

    def take(unit, pieces):
        for piece in pieces:
            await_copy(unit_ref(origin(piece, core), unit), u_recv.at[piece, unit])

    def to_twin(unit, pieces):
        for piece in pieces:
            go(unit_ref(origin(piece, core), unit), twin_recv.at[piece, unit], twin_device)

    def relay_first(unit):
        take(unit, (AHEAD, BEHIND, ACROSS))
        go(unit_ref(place(0, -sign, core), unit), u_recv.at[FAR, unit], sign_device)
        pass_on(ACROSS, unit, NEAR_ACROSS, back_device)
        to_twin(unit, (AHEAD, BEHIND, ACROSS))

    def relay_second(unit):
        take(unit, (FAR, NEAR_ACROSS))
        pass_on(FAR, unit, FAR_ACROSS, across_device)
        pass_on(NEAR_ACROSS, unit, OTHER_ACROSS, below_device if unit == 1 else above_device)
        to_twin(unit, (FAR, NEAR_ACROSS))

    def relay_third(unit):
        take(unit, (OTHER_ACROSS, FAR_ACROSS))
        to_twin(unit, (OTHER_ACROSS, FAR_ACROSS))

    def relay_keys():
        for piece in range(1, 8):
            await_copy(k_ref(piece, core), k_recv.at[piece])
            go(k_ref(piece, core), kt_recv.at[piece], twin_device)

    def arrive(unit):
        for piece in range(8):
            await_copy(unit_ref(origin(piece, 1 - core), unit), twin_recv.at[piece, unit])

    kv_in.wait()
    both = kv_ref[...].astype(F32)
    kv[tok] = jnp.concatenate(
        [both[0, :, :HALF], both[1, :, :HALF], both[0, :, HALF:], both[1, :, HALF:]], axis=0
    ).astype(BF16)
    qg_in.wait()
    atoms_in.wait()
    out_in.wait()
    slot_in.wait()
    tokens = iota((3 * TOK, WIDTH), 0) + (me - 1) * TOK
    for b in range(ROWS // WIDTH):
        named = slot_ref[b : b + 1, :]
        oh[:, b * WIDTH : (b + 1) * WIDTH] = (tokens == named).astype(F32).astype(BF16)
    span8 = 8 * KEYS
    member = lax.div(iota((span8, HALF), 0), KEYS) == lax.div(iota((span8, HALF), 1), HEAD)
    mbd[...] = member.astype(F32).astype(BF16)
    if comm:
        pl.semaphore_wait(barrier, len(peers))
    direct(0)
    last, first = pl.ds(ROWS, RIM), pl.ds(RIM, RIM)
    low, high = pl.ds(0, RIM), pl.ds(ROWS + RIM, RIM)
    go(ap.at[last], halo_recv.at[0], right_device, ap.at[low])
    go(ap.at[first], halo_recv.at[1], left_device, ap.at[high])
    for piece in range(1, 8):
        go(k_ref(0, core), k_recv.at[piece], targets[piece])
    go(k_ref(OWN, core), kt_recv.at[OWN], twin_device)
    for unit in range(3):
        to_twin(unit, (OWN,))

    def project(start, count, with_queries):
        values = ap[pl.ds(start, count), :].astype(F32)
        normed = layer_norm(values, atom_gain_ref[...]).astype(BF16)
        projected = mm(normed, qkv_ref[...]).astype(BF16)
        if with_queries:
            qs[pl.ds(start - RIM, count), :] = projected[:, :WIDTH]
        ks[pl.ds(start, count), :] = projected[:, WIDTH : 2 * WIDTH]
        vs[pl.ds(start, count), 0:WIDTH] = projected[:, 2 * WIDTH :]
        vs[pl.ds(start, count), WIDTH : 2 * WIDTH] = jnp.ones((count, WIDTH), BF16)

    gain_in.wait()
    qkv_in.wait()
    for part in range(5):
        project(RIM + part * 256, 256, True)

    direct(1)
    lane = iota((QWIN, WIDTH), 1)
    head_of_lane = lax.div(lane, 32)
    head_masks = [(head_of_lane == h).astype(F32).astype(BF16) for h in range(ATOM_HEADS)]
    mix_row = iota((KWIN, KWIN), 0)
    mix_col = iota((KWIN, KWIN), 1)
    source = lax.rem(mix_row, QWIN) * ATOM_HEADS + lax.div(mix_row, QWIN)
    reorder = (mix_col == source).astype(F32).astype(BF16)
    scale = 32 ** (-0.5)
    low_end = jnp.where(me == 0, RIM, 0)
    high_end = jnp.where(me == 31, ROWS + RIM, PADDED)

    def window(w, edge):
        start = pl.multiple_of(w * QWIN, QWIN)
        queries = qs[pl.ds(start, QWIN), :]
        expanded = jnp.concatenate([queries * mask for mask in head_masks], axis=0)
        scores = mm(expanded, kt[w]) * scale
        scores += mm(reorder, bias[pl.ds(start * ATOM_HEADS, KWIN), :])
        if edge:
            place_of_key = start + mix_col
            inside = (place_of_key >= low_end) & (place_of_key < high_end)
            scores = jnp.where(inside, scores, -1e30)
        largest = jnp.max(scores, axis=1, keepdims=True)
        weights = jnp.exp(scores - largest).astype(BF16)
        both = mm(weights, vs[pl.ds(start, KWIN), :])
        rows = [both[h * QWIN : (h + 1) * QWIN] for h in range(ATOM_HEADS)]
        mixed, totals = rows[0][:, :WIDTH], rows[0][:, WIDTH:]
        for h in range(1, ATOM_HEADS):
            mixed = jnp.where(head_of_lane == h, rows[h][:, :WIDTH], mixed)
            totals = jnp.where(head_of_lane == h, rows[h][:, WIDTH:], totals)
        mx[pl.ds(start, QWIN), :] = (mixed / totals).astype(BF16)

    def transposed_keys(w):
        kt[w] = ks[pl.ds(pl.multiple_of(w * QWIN, QWIN), KWIN), :].T

    def turn(i, carry):
        for u in range(6):
            transposed_keys(6 * i + 2 + u)
        return carry

    lax.fori_loop(0, 6, turn, 0)
    direct(2)
    bias_in.wait()

    def interior(i, carry):
        for u in range(8):
            window(8 * i + 2 + u, False)
        return carry

    lax.fori_loop(0, 2, interior, 0)
    relay_first(0)
    lax.fori_loop(2, 4, interior, 0)

    relay_first(1)
    await_copy(ap.at[low], halo_recv.at[0])
    await_copy(ap.at[high], halo_recv.at[1])
    project(0, RIM, False)
    project(ROWS + RIM, RIM, False)
    for w in (38, 39, 0, 1):
        transposed_keys(w)
    for w in (34, 35, 36, 37):
        window(w, False)
    for w in (38, 39, 0, 1):
        window(w, True)

    relay_first(2)
    for copy in small_in:
        copy.wait()
    for part in range(5):
        span = pl.ds(part * 256, 256)
        values = ap[pl.ds(RIM + part * 256, 256), :].astype(F32)
        up[span, :] = (values + mm(mx[span, :], atom_out_ref[...])).astype(BF16)

    relay_second(0)
    for c in range(CHUNKS):
        columns = slice(c * CHUNK, (c + 1) * CHUNK)
        for part in range(5):
            span = pl.ds(part * 256, 256)
            lf[c, span, :] = jnp.maximum(mm(up[span, :], agg_ref[:, columns]), 0.0).astype(BF16)
        lifted = lf[c]
        sb[0, c] = mm(oh[0:TOK, :], lifted).astype(BF16)
        sb[1, c] = mm(oh[2 * TOK : 3 * TOK, :], lifted).astype(BF16)
        go(sb.at[0, c], x_recv.at[0, c], left_device, rb.at[0, c])
        go(sb.at[1, c], x_recv.at[1, c], right_device, rb.at[1, c])
    relay_second(1)
    for c in range(CHUNKS):
        own_sum[:, c * CHUNK : (c + 1) * CHUNK] = mm(oh[TOK : 2 * TOK, :], lf[c])

    pair_in.wait()
    pair_weights = pair_weight_ref[...]

    def pair_bias(i, carry):
        for u in range(4):
            j = i * 8 + u * 2
            features = jnp.concatenate(
                [pair[j], pair[j + TOK // 2], pair[j + 1], pair[j + 1 + TOK // 2]], axis=0
            )
            both = mm_nt(pair_weights, features)
            start = pl.multiple_of(j * HEADS, 2 * HEADS)
            raw[pl.ds(start, HEADS), :] = both[:, :WIDTH]
            raw[pl.ds(start + HEADS, HEADS), :] = both[:, WIDTH:]
        return carry

    lax.fori_loop(0, 4, pair_bias, 0)
    relay_second(2)
    lax.fori_loop(4, 8, pair_bias, 0)
    relay_third(0)
    relay_keys()
    half = TOK // 2
    first_key = iota((half, WIDTH), 1) < KEYS
    for g in range(HEADS // 2):
        even = raw[pl.ds(2 * g, half, stride=HEADS), :]
        odd = raw[pl.ds(2 * g + 1, half, stride=HEADS), :]
        columns = slice(g * WIDTH, (g + 1) * WIDTH)
        tb[0:half, columns] = jnp.where(first_key, even, pltpu.roll(odd, KEYS, 1)).astype(BF16)
        tb[half:TOK, columns] = jnp.where(first_key, pltpu.roll(even, KEYS, 1), odd).astype(BF16)

    relay_third(1)
    for piece in range(8):
        await_copy(k_ref(piece, 1 - core), kt_recv.at[piece])
    gathered = kv[...].astype(F32)
    for g in range(2):
        keys = gathered[:, 8 * g : 8 * g + 4, :].reshape(KEYS, HALF).astype(BF16)
        values = gathered[:, 8 * g + 4 : 8 * g + 8, :].reshape(KEYS, HALF).astype(BF16)
        for h in range(8):
            span = slice(h * KEYS, (h + 1) * KEYS)
            vbd[g, span, :] = values * mbd[span, :]
        kbd[g] = (jnp.concatenate([keys] * 8, axis=0) * mbd[...]).T

    relay_third(2)
    single_in.wait()
    for c in range(CHUNKS):
        for side in range(2):
            await_copy(rb.at[side, c], x_recv.at[side, c])
    counts = jnp.broadcast_to(count_ref[...].astype(F32), (TOK, TOK)).T
    inverse = 1.0 / counts
    for c in range(CHUNKS):
        columns = slice(c * CHUNK, (c + 1) * CHUNK)
        sums = own_sum[:, columns] + rb[0, c].astype(F32) + rb[1, c].astype(F32)
        per = jnp.concatenate([inverse, inverse], axis=1)
        acts[:, columns] = sums * per + single[:, columns].astype(F32)
    gain = jnp.concatenate([token_gain_ref[i : i + 1, :] for i in range(CH // WIDTH)], axis=1)
    normed = layer_norm(acts[...], gain).astype(BF16)

    arrive(0)
    arrive(1)
    queries = mm_nt(normed, wq[0]).astype(BF16)
    gates = jax.nn.sigmoid(mm_nt(normed, wq[1]))

    token_scale = HEAD ** (-0.5)
    low = iota((TOK, WIDTH), 1) < KEYS
    gated = []
    for g in range(2):
        columns = slice(g * HALF, (g + 1) * HALF)
        scores = mm(queries[:, columns], kbd[g]) * token_scale
        scores += tb[:, g * span8 : (g + 1) * span8].astype(F32)
        weights = []
        for i in range(4):
            part = scores[:, i * WIDTH : (i + 1) * WIDTH]
            top_low = jnp.max(jnp.where(low, part, -jnp.inf), axis=1, keepdims=True)
            top_high = jnp.max(jnp.where(low, -jnp.inf, part), axis=1, keepdims=True)
            weights.append(jnp.exp(part - jnp.where(low, top_low, top_high)).astype(BF16))
        weights = jnp.concatenate(weights, axis=1)
        mixed = mm(weights, vbd[g]) / mm(weights, mbd[...])
        gated.append((gates[:, columns] * mixed).astype(BF16))
    gated = jnp.concatenate(gated, axis=1)

    arrive(2)
    tu[...] = (acts[...] + mm(gated, wo[...])).astype(BF16)
    for copy in started:
        copy.wait_send()


def call(comm, *args):
    hbm = pl.BlockSpec(memory_space=pl.ANY)
    v = pltpu.VMEM
    dma = pltpu.SemaphoreType.DMA
    return pl.pallas_call(
        functools.partial(kernel, comm),
        out_shape=(v((ROWS, WIDTH), BF16), v((TOK, CH), BF16)),
        in_specs=[hbm] * 15,
        out_specs=(pl.BlockSpec(memory_space=v), pl.BlockSpec(memory_space=v)),
        scratch_shapes=[
            v((PADDED, WIDTH), BF16),
            v((ROWS * ATOM_HEADS, KWIN), BF16),
            v((TOK, CH), BF16),
            v((TOK, KEYS, WIDTH), BF16),
            v((ROWS, WIDTH), BF16),
            v((PADDED, WIDTH), BF16),
            v((WINDOWS, WIDTH, KWIN), BF16),
            v((PADDED, 2 * WIDTH), BF16),
            v((ROWS, WIDTH), BF16),
            v((3 * TOK, ROWS), BF16),
            v((CHUNKS, ROWS, CHUNK), BF16),
            v((TOK, CH), F32),
            v((2, CHUNKS, TOK, CHUNK), BF16),
            v((2, CHUNKS, TOK, CHUNK), BF16),
            v((2, CH, CH), BF16),
            v((CH, CH), BF16),
            v((HEADS, 16, CH // 2), BF16),
            v((TOK // 2 * HEADS, WIDTH), F32),
            v((TOK, HEADS * KEYS), BF16),
            v((2, HALF, 8 * KEYS), BF16),
            v((2, 8 * KEYS, HALF), BF16),
            v((8 * KEYS, CH // 2), BF16),
            v((TOK, CH), F32),
            v((ROWS // WIDTH, WIDTH), jnp.int32),
            v((1, TOK), jnp.int32),
            v((2, 4, CH), BF16),
            v((1, WIDTH), F32),
            v((WIDTH, 3 * WIDTH), BF16),
            v((WIDTH, WIDTH), BF16),
            v((WIDTH, CH), BF16),
            v((CH // WIDTH, WIDTH), F32),
            v((HEADS, WIDTH), BF16),
            dma((17,)),
            dma((80,)),
            dma((2,)),
            dma((8, 3,)),
            dma((8, 3,)),
            dma((8,)),
            dma((8,)),
            dma((2, CHUNKS)),
        ],
        compiler_params=pltpu.CompilerParams(
            collective_id=0 if comm else None,
            has_side_effects=True,
            vmem_limit_bytes=60 * 1024 * 1024,
        ),
    )(*args)


def write_kernel(up, tu, atom_update, token_update, sems):
    copies = [
        pltpu.make_async_copy(up, atom_update, sems.at[0]),
        pltpu.make_async_copy(tu, token_update, sems.at[1]),
    ]
    for copy in copies:
        copy.start()
    for copy in copies:
        copy.wait()


def write(up, tu):
    hbm = pl.BlockSpec(memory_space=pl.ANY)
    return pl.pallas_call(
        write_kernel,
        out_shape=(
            jax.ShapeDtypeStruct((ROWS, WIDTH), BF16),
            jax.ShapeDtypeStruct((TOK, CH), BF16),
        ),
        in_specs=[pl.BlockSpec(memory_space=pltpu.VMEM)] * 2,
        out_specs=(hbm, hbm),
        scratch_shapes=[pltpu.SemaphoreType.DMA((2,))],
        compiler_params=pltpu.CompilerParams(vmem_limit_bytes=8 * 1024 * 1024),
    )(up, tu)


def body(
    atoms,
    atom_bias,
    atom_token,
    token_atoms,
    token_single,
    key_value,
    pair,
    atom_gain,
    atom_qkv,
    atom_out_weight,
    agg_weight,
    token_gain,
    query_gate_weight,
    pair_weight,
    out_weight,
    comm=True,
):
    up, tu = call(
        comm,
        atoms,
        atom_bias.reshape(ROWS * ATOM_HEADS, KWIN),
        atom_token.reshape(ROWS // WIDTH, WIDTH),
        token_atoms.reshape(1, TOK),
        token_single,
        key_value,
        pair,
        atom_gain.reshape(1, WIDTH),
        atom_qkv,
        atom_out_weight,
        agg_weight,
        token_gain.reshape(CH // WIDTH, WIDTH),
        query_gate_weight.transpose(0, 2, 1),
        pair_weight.T,
        out_weight,
    )
    return write(up, tu)


def solution(mesh):
    return jax.shard_map(
        body,
        mesh=mesh,
        in_specs=(
            P(("tok", "atom"), None),
            P(("tok", "atom"), None, None),
            P(("tok", "atom")),
            P(("tok", "atom")),
            P(("tok", "atom"), None),
            P(None, "tok", None),
            P(("tok", "atom"), None, None),
            P(),
            P(),
            P(),
            P(),
            P(),
            P(None, None, "tok"),
            P(),
            P("tok", None),
        ),
        out_specs=(P(("tok", "atom"), None), P(("tok", "atom"), None)),
        check_vma=False,
    )
```

```python
import functools

import jax
import jax.numpy as jnp
from jax import lax
from jax.experimental import pallas as pl
from jax.experimental.pallas import tpu as pltpu
from jax.sharding import PartitionSpec as P

MESH = pl.DeviceIdType.MESH
F32 = jnp.float32
BF16 = jnp.bfloat16

ATOM_HEADS = 4
QWIN = 32
KWIN = 128
RIM = 48
ROWS = 1280
PADDED = ROWS + 2 * RIM
WINDOWS = ROWS // QWIN
WIDTH = 128
TOK = 128
CH = 768
HEADS = 16
HEAD = 48
HALF = CH // 2
KEYS = 64
CHUNKS = 3
CHUNK = CH // CHUNKS
EPSILON = 1e-05
PIECES = ((0, 0), (0, 1), (0, -1), (1, 0), (0, 2), (1, 1), (1, -1), (1, 2))
OWN, AHEAD, BEHIND, ACROSS, FAR, NEAR_ACROSS, OTHER_ACROSS, FAR_ACROSS = range(8)
NT = (((1,), (1,)), ((), ()))


def mm(a, b):
    return jnp.dot(a, b, preferred_element_type=F32)


def mm_nt(a, b):
    return lax.dot_general(a, b, NT, preferred_element_type=F32)


def iota(shape, axis):
    return lax.broadcasted_iota(jnp.int32, shape, axis)


def layer_norm(values, gain):
    centre = values - jnp.mean(values, axis=-1, keepdims=True)
    spread = jnp.mean(centre * centre, axis=-1, keepdims=True)
    return centre * lax.rsqrt(spread + EPSILON) * gain


def kernel(
    comm,
    atoms_hbm,
    bias_hbm,
    slot_hbm,
    count_hbm,
    single_hbm,
    kv_hbm,
    pair_hbm,
    atom_gain_hbm,
    qkv_hbm,
    atom_out_hbm,
    agg_hbm,
    token_gain_hbm,
    qg_hbm,
    pair_weight_hbm,
    out_hbm,
    up,
    tu,
    ap,
    bias,
    single,
    pair,
    qs,
    ks,
    kt,
    vs,
    mx,
    oh,
    lf,
    own_sum,
    sb,
    rb,
    wq,
    wo,
    kv,
    raw,
    tb,
    kbd,
    vbd,
    mbd,
    acts,
    slot_ref,
    count_ref,
    kv_ref,
    atom_gain_ref,
    qkv_ref,
    atom_out_ref,
    agg_ref,
    token_gain_ref,
    pair_weight_ref,
    local_sem,
    send_sem,
    halo_recv,
    u_recv,
    twin_recv,
    x_recv,
):
    if comm:
        tok = lax.axis_index("tok")
        me = lax.axis_index("atom")
    else:
        tok = jnp.int32(5)
        me = jnp.int32(7)
    core = lax.rem(tok, 2)
    row = lax.rem(lax.div(tok, 2), 4)
    hi = lax.div(tok, 8)
    lo = lax.rem(me, 2)
    left = lax.rem(me + 31, 32)
    right = lax.rem(me + 1, 32)
    twin = tok + 1 - 2 * core

    def place(flip, step, who):
        high = 1 - hi if flip else hi
        return (high * 4 + lax.rem(row + step + 4, 4)) * 2 + who

    sign = 1 - 2 * lax.rem(lax.div(me, 2), 2)

    def origin(piece, who):
        flip, step = PIECES[piece]
        return place(flip, step if piece < FAR else sign * step, who)

    across = me + 1 - 2 * lo
    up_device = (place(0, 1, core), me)
    down_device = (place(0, -1, core), me)
    across_device = (place(1, 0, core), across)
    twin_device = (twin, me)
    left_device = (tok, left)
    right_device = (tok, right)
    sign_device = (place(0, sign, core), me)
    back_device = (place(0, -sign, core), me)
    above_device = (tok, lax.rem(me + 2, 32))
    below_device = (tok, lax.rem(me + 30, 32))
    peers = [up_device, down_device, across_device, twin_device, left_device, right_device, above_device, below_device]
    if comm:
        barrier = pltpu.get_barrier_semaphore()
        for peer in peers:
            pl.semaphore_signal(barrier, inc=1, device_id=peer, device_id_type=MESH)

    def local(i, src, dst):
        copy = pltpu.make_async_copy(src, dst, local_sem.at[i])
        copy.start()
        return copy

    def block(which):
        return pl.ds(pl.multiple_of(which * HEAD, 16), HEAD)

    qg_in = local(7, qg_hbm, wq.at[:, block(tok), :])
    out_in = local(1, out_hbm, wo.at[block(tok)])
    kv_in = local(8, kv_hbm, kv_ref)
    atoms_in = local(0, atoms_hbm, ap.at[pl.ds(RIM, ROWS)])
    gain_in = local(9, atom_gain_hbm, atom_gain_ref)
    qkv_in = local(10, qkv_hbm, qkv_ref)
    slot_in = local(13, slot_hbm, slot_ref)
    bias_in = local(2, bias_hbm, bias)
    small_in = [
        local(11, atom_out_hbm, atom_out_ref),
        local(12, agg_hbm, agg_ref),
        local(14, count_hbm, count_ref),
        local(15, token_gain_hbm, token_gain_ref),
        local(16, pair_weight_hbm, pair_weight_ref),
    ]
    pair_in = local(3, pair_hbm, pair)
    single_in = local(4, single_hbm, single)

    started = []

    def send(src, dst, recv, device):
        return pltpu.make_async_remote_copy(
            src_ref=src, dst_ref=dst, send_sem=send_sem.at[len(started)], recv_sem=recv,
            device_id=device, device_id_type=MESH,
        )

    def go(ref, recv, device, target=None):
        if comm:
            copy = send(ref, ref if target is None else target, recv, device)
            copy.start()
            started.append(copy)

    def await_copy(ref, recv):
        if comm:
            send(ref, ref, recv, twin_device).wait_recv()

    def unit_ref(tok_of, unit):
        if unit == 3:
            return kv.at[tok_of]
        return wq.at[unit, block(tok_of), :] if unit < 2 else wo.at[block(tok_of)]

    def pass_on(piece, unit, name, device):
        go(unit_ref(origin(piece, core), unit), u_recv.at[name, unit], device)

    def direct(unit):
        pass_on(OWN, unit, BEHIND, up_device)
        pass_on(OWN, unit, AHEAD, down_device)
        pass_on(OWN, unit, ACROSS, across_device)

    def take(unit, pieces):
        for piece in pieces:
            await_copy(unit_ref(origin(piece, core), unit), u_recv.at[piece, unit])

    def to_twin(unit, pieces):
        for piece in pieces:
            go(unit_ref(origin(piece, core), unit), twin_recv.at[piece, unit], twin_device)

    def relay_first(unit):
        take(unit, (AHEAD, BEHIND, ACROSS))
        go(unit_ref(place(0, -sign, core), unit), u_recv.at[FAR, unit], sign_device)
        pass_on(ACROSS, unit, NEAR_ACROSS, back_device)
        to_twin(unit, (AHEAD, BEHIND, ACROSS))

    def relay_second(unit):
        take(unit, (FAR, NEAR_ACROSS))
        pass_on(FAR, unit, FAR_ACROSS, across_device)
        pass_on(NEAR_ACROSS, unit, OTHER_ACROSS, below_device if unit == 1 else above_device)
        to_twin(unit, (FAR, NEAR_ACROSS))

    def relay_third(unit):
        take(unit, (OTHER_ACROSS, FAR_ACROSS))
        to_twin(unit, (OTHER_ACROSS, FAR_ACROSS))

    def arrive(unit):
        for piece in range(8):
            await_copy(unit_ref(origin(piece, 1 - core), unit), twin_recv.at[piece, unit])

    kv_in.wait()
    both = kv_ref[...].astype(F32)
    kv[tok] = jnp.concatenate(
        [both[0, :, :HALF], both[1, :, :HALF], both[0, :, HALF:], both[1, :, HALF:]], axis=0
    ).astype(BF16)
    qg_in.wait()
    atoms_in.wait()
    out_in.wait()
    slot_in.wait()
    tokens = iota((3 * TOK, WIDTH), 0) + (me - 1) * TOK
    for b in range(ROWS // WIDTH):
        named = slot_ref[b : b + 1, :]
        oh[:, b * WIDTH : (b + 1) * WIDTH] = (tokens == named).astype(F32).astype(BF16)
    span8 = 8 * KEYS
    member = lax.div(iota((span8, HALF), 0), KEYS) == lax.div(iota((span8, HALF), 1), HEAD)
    mbd[...] = member.astype(F32).astype(BF16)
    if comm:
        pl.semaphore_wait(barrier, len(peers))
    direct(0)
    last, first = pl.ds(ROWS, RIM), pl.ds(RIM, RIM)
    low, high = pl.ds(0, RIM), pl.ds(ROWS + RIM, RIM)
    go(ap.at[last], halo_recv.at[0], right_device, ap.at[low])
    go(ap.at[first], halo_recv.at[1], left_device, ap.at[high])

    def project(start, count, with_queries):
        values = ap[pl.ds(start, count), :].astype(F32)
        normed = layer_norm(values, atom_gain_ref[...]).astype(BF16)
        projected = mm(normed, qkv_ref[...]).astype(BF16)
        if with_queries:
            qs[pl.ds(start - RIM, count), :] = projected[:, :WIDTH]
        ks[pl.ds(start, count), :] = projected[:, WIDTH : 2 * WIDTH]
        vs[pl.ds(start, count), 0:WIDTH] = projected[:, 2 * WIDTH :]
        vs[pl.ds(start, count), WIDTH : 2 * WIDTH] = jnp.ones((count, WIDTH), BF16)

    gain_in.wait()
    qkv_in.wait()
    for part in range(5):
        project(RIM + part * 256, 256, True)

    direct(1)
    lane = iota((QWIN, WIDTH), 1)
    head_of_lane = lax.div(lane, 32)
    head_masks = [(head_of_lane == h).astype(F32).astype(BF16) for h in range(ATOM_HEADS)]
    mix_row = iota((KWIN, KWIN), 0)
    mix_col = iota((KWIN, KWIN), 1)
    source = lax.rem(mix_row, QWIN) * ATOM_HEADS + lax.div(mix_row, QWIN)
    reorder = (mix_col == source).astype(F32).astype(BF16)
    scale = 32 ** (-0.5)
    low_end = jnp.where(me == 0, RIM, 0)
    high_end = jnp.where(me == 31, ROWS + RIM, PADDED)

    def window(w, edge):
        start = pl.multiple_of(w * QWIN, QWIN)
        queries = qs[pl.ds(start, QWIN), :]
        expanded = jnp.concatenate([queries * mask for mask in head_masks], axis=0)
        scores = mm(expanded, kt[w]) * scale
        scores += mm(reorder, bias[pl.ds(start * ATOM_HEADS, KWIN), :])
        if edge:
            place_of_key = start + mix_col
            inside = (place_of_key >= low_end) & (place_of_key < high_end)
            scores = jnp.where(inside, scores, -1e30)
        largest = jnp.max(scores, axis=1, keepdims=True)
        weights = jnp.exp(scores - largest).astype(BF16)
        both = mm(weights, vs[pl.ds(start, KWIN), :])
        rows = [both[h * QWIN : (h + 1) * QWIN] for h in range(ATOM_HEADS)]
        mixed, totals = rows[0][:, :WIDTH], rows[0][:, WIDTH:]
        for h in range(1, ATOM_HEADS):
            mixed = jnp.where(head_of_lane == h, rows[h][:, :WIDTH], mixed)
            totals = jnp.where(head_of_lane == h, rows[h][:, WIDTH:], totals)
        mx[pl.ds(start, QWIN), :] = (mixed / totals).astype(BF16)

    def transposed_keys(w):
        kt[w] = ks[pl.ds(pl.multiple_of(w * QWIN, QWIN), KWIN), :].T

    def turn(i, carry):
        for u in range(6):
            transposed_keys(6 * i + 2 + u)
        return carry

    lax.fori_loop(0, 6, turn, 0)
    direct(3)
    direct(2)
    bias_in.wait()

    def interior(i, carry):
        for u in range(8):
            window(8 * i + 2 + u, False)
        return carry

    lax.fori_loop(0, 2, interior, 0)
    relay_first(0)
    for unit in range(4):
        to_twin(unit, (OWN,))
    lax.fori_loop(2, 4, interior, 0)

    relay_first(1)
    await_copy(ap.at[low], halo_recv.at[0])
    await_copy(ap.at[high], halo_recv.at[1])
    project(0, RIM, False)
    project(ROWS + RIM, RIM, False)
    for w in (38, 39, 0, 1):
        transposed_keys(w)
    for w in (34, 35, 36, 37):
        window(w, False)
    for w in (38, 39, 0, 1):
        window(w, True)

    relay_first(3)
    relay_first(2)
    for copy in small_in:
        copy.wait()
    for part in range(5):
        span = pl.ds(part * 256, 256)
        values = ap[pl.ds(RIM + part * 256, 256), :].astype(F32)
        up[span, :] = (values + mm(mx[span, :], atom_out_ref[...])).astype(BF16)

    relay_second(0)
    for c in range(CHUNKS):
        columns = slice(c * CHUNK, (c + 1) * CHUNK)
        for part in range(5):
            span = pl.ds(part * 256, 256)
            lf[c, span, :] = jnp.maximum(mm(up[span, :], agg_ref[:, columns]), 0.0).astype(BF16)
        lifted = lf[c]
        sb[0, c] = mm(oh[0:TOK, :], lifted).astype(BF16)
        sb[1, c] = mm(oh[2 * TOK : 3 * TOK, :], lifted).astype(BF16)
        go(sb.at[0, c], x_recv.at[0, c], left_device, rb.at[0, c])
        go(sb.at[1, c], x_recv.at[1, c], right_device, rb.at[1, c])
    relay_second(1)
    relay_second(3)
    for c in range(CHUNKS):
        own_sum[:, c * CHUNK : (c + 1) * CHUNK] = mm(oh[TOK : 2 * TOK, :], lf[c])

    pair_in.wait()
    pair_weights = pair_weight_ref[...]

    def pair_bias(i, carry):
        for u in range(4):
            j = i * 8 + u * 2
            features = jnp.concatenate(
                [pair[j], pair[j + TOK // 2], pair[j + 1], pair[j + 1 + TOK // 2]], axis=0
            )
            both = mm_nt(pair_weights, features)
            start = pl.multiple_of(j * HEADS, 2 * HEADS)
            raw[pl.ds(start, HEADS), :] = both[:, :WIDTH]
            raw[pl.ds(start + HEADS, HEADS), :] = both[:, WIDTH:]
        return carry

    lax.fori_loop(0, 4, pair_bias, 0)
    relay_second(2)
    lax.fori_loop(4, 8, pair_bias, 0)
    relay_third(0)
    relay_third(3)
    half = TOK // 2
    first_key = iota((half, WIDTH), 1) < KEYS
    for g in range(HEADS // 2):
        even = raw[pl.ds(2 * g, half, stride=HEADS), :]
        odd = raw[pl.ds(2 * g + 1, half, stride=HEADS), :]
        columns = slice(g * WIDTH, (g + 1) * WIDTH)
        tb[0:half, columns] = jnp.where(first_key, even, pltpu.roll(odd, KEYS, 1)).astype(BF16)
        tb[half:TOK, columns] = jnp.where(first_key, pltpu.roll(even, KEYS, 1), odd).astype(BF16)

    relay_third(1)
    arrive(3)
    gathered = kv[...].astype(F32)
    for g in range(2):
        keys = gathered[:, 8 * g : 8 * g + 4, :].reshape(KEYS, HALF).astype(BF16)
        values = gathered[:, 8 * g + 4 : 8 * g + 8, :].reshape(KEYS, HALF).astype(BF16)
        for h in range(8):
            span = slice(h * KEYS, (h + 1) * KEYS)
            vbd[g, span, :] = values * mbd[span, :]
        kbd[g] = (jnp.concatenate([keys] * 8, axis=0) * mbd[...]).T

    relay_third(2)
    single_in.wait()
    for c in range(CHUNKS):
        for side in range(2):
            await_copy(rb.at[side, c], x_recv.at[side, c])
    counts = jnp.broadcast_to(count_ref[...].astype(F32), (TOK, TOK)).T
    inverse = 1.0 / counts
    for c in range(CHUNKS):
        columns = slice(c * CHUNK, (c + 1) * CHUNK)
        sums = own_sum[:, columns] + rb[0, c].astype(F32) + rb[1, c].astype(F32)
        per = jnp.concatenate([inverse, inverse], axis=1)
        acts[:, columns] = sums * per + single[:, columns].astype(F32)
    gain = jnp.concatenate([token_gain_ref[i : i + 1, :] for i in range(CH // WIDTH)], axis=1)
    normed = layer_norm(acts[...], gain).astype(BF16)

    arrive(0)
    arrive(1)
    queries = mm_nt(normed, wq[0]).astype(BF16)
    gates = jax.nn.sigmoid(mm_nt(normed, wq[1]))

    token_scale = HEAD ** (-0.5)
    low = iota((TOK, WIDTH), 1) < KEYS
    gated = []
    for g in range(2):
        columns = slice(g * HALF, (g + 1) * HALF)
        scores = mm(queries[:, columns], kbd[g]) * token_scale
        scores += tb[:, g * span8 : (g + 1) * span8].astype(F32)
        weights = []
        for i in range(4):
            part = scores[:, i * WIDTH : (i + 1) * WIDTH]
            top_low = jnp.max(jnp.where(low, part, -jnp.inf), axis=1, keepdims=True)
            top_high = jnp.max(jnp.where(low, -jnp.inf, part), axis=1, keepdims=True)
            weights.append(jnp.exp(part - jnp.where(low, top_low, top_high)).astype(BF16))
        weights = jnp.concatenate(weights, axis=1)
        mixed = mm(weights, vbd[g]) / mm(weights, mbd[...])
        gated.append((gates[:, columns] * mixed).astype(BF16))
    gated = jnp.concatenate(gated, axis=1)

    arrive(2)
    tu[...] = (acts[...] + mm(gated, wo[...])).astype(BF16)
    for copy in started:
        copy.wait_send()


def call(comm, *args):
    hbm = pl.BlockSpec(memory_space=pl.ANY)
    v = pltpu.VMEM
    dma = pltpu.SemaphoreType.DMA
    return pl.pallas_call(
        functools.partial(kernel, comm),
        out_shape=(v((ROWS, WIDTH), BF16), v((TOK, CH), BF16)),
        in_specs=[hbm] * 15,
        out_specs=(pl.BlockSpec(memory_space=v), pl.BlockSpec(memory_space=v)),
        scratch_shapes=[
            v((PADDED, WIDTH), BF16),
            v((ROWS * ATOM_HEADS, KWIN), BF16),
            v((TOK, CH), BF16),
            v((TOK, KEYS, WIDTH), BF16),
            v((ROWS, WIDTH), BF16),
            v((PADDED, WIDTH), BF16),
            v((WINDOWS, WIDTH, KWIN), BF16),
            v((PADDED, 2 * WIDTH), BF16),
            v((ROWS, WIDTH), BF16),
            v((3 * TOK, ROWS), BF16),
            v((CHUNKS, ROWS, CHUNK), BF16),
            v((TOK, CH), F32),
            v((2, CHUNKS, TOK, CHUNK), BF16),
            v((2, CHUNKS, TOK, CHUNK), BF16),
            v((2, CH, CH), BF16),
            v((CH, CH), BF16),
            v((HEADS, 16, CH // 2), BF16),
            v((TOK // 2 * HEADS, WIDTH), F32),
            v((TOK, HEADS * KEYS), BF16),
            v((2, HALF, 8 * KEYS), BF16),
            v((2, 8 * KEYS, HALF), BF16),
            v((8 * KEYS, CH // 2), BF16),
            v((TOK, CH), F32),
            v((ROWS // WIDTH, WIDTH), jnp.int32),
            v((1, TOK), jnp.int32),
            v((2, 4, CH), BF16),
            v((1, WIDTH), F32),
            v((WIDTH, 3 * WIDTH), BF16),
            v((WIDTH, WIDTH), BF16),
            v((WIDTH, CH), BF16),
            v((CH // WIDTH, WIDTH), F32),
            v((HEADS, WIDTH), BF16),
            dma((17,)),
            dma((80,)),
            dma((2,)),
            dma((8, 4)),
            dma((8, 4)),
            dma((2, CHUNKS)),
        ],
        compiler_params=pltpu.CompilerParams(
            collective_id=0 if comm else None,
            has_side_effects=True,
            vmem_limit_bytes=60 * 1024 * 1024,
        ),
    )(*args)


def write_kernel(up, tu, atom_update, token_update, sems):
    copies = [
        pltpu.make_async_copy(up, atom_update, sems.at[0]),
        pltpu.make_async_copy(tu, token_update, sems.at[1]),
    ]
    for copy in copies:
        copy.start()
    for copy in copies:
        copy.wait()


def write(up, tu):
    hbm = pl.BlockSpec(memory_space=pl.ANY)
    return pl.pallas_call(
        write_kernel,
        out_shape=(
            jax.ShapeDtypeStruct((ROWS, WIDTH), BF16),
            jax.ShapeDtypeStruct((TOK, CH), BF16),
        ),
        in_specs=[pl.BlockSpec(memory_space=pltpu.VMEM)] * 2,
        out_specs=(hbm, hbm),
        scratch_shapes=[pltpu.SemaphoreType.DMA((2,))],
        compiler_params=pltpu.CompilerParams(vmem_limit_bytes=8 * 1024 * 1024),
    )(up, tu)


def body(
    atoms,
    atom_bias,
    atom_token,
    token_atoms,
    token_single,
    key_value,
    pair,
    atom_gain,
    atom_qkv,
    atom_out_weight,
    agg_weight,
    token_gain,
    query_gate_weight,
    pair_weight,
    out_weight,
    comm=True,
):
    up, tu = call(
        comm,
        atoms,
        atom_bias.reshape(ROWS * ATOM_HEADS, KWIN),
        atom_token.reshape(ROWS // WIDTH, WIDTH),
        token_atoms.reshape(1, TOK),
        token_single,
        key_value,
        pair,
        atom_gain.reshape(1, WIDTH),
        atom_qkv,
        atom_out_weight,
        agg_weight,
        token_gain.reshape(CH // WIDTH, WIDTH),
        query_gate_weight.transpose(0, 2, 1),
        pair_weight.T,
        out_weight,
    )
    return write(up, tu)


def solution(mesh):
    return jax.shard_map(
        body,
        mesh=mesh,
        in_specs=(
            P(("tok", "atom"), None),
            P(("tok", "atom"), None, None),
            P(("tok", "atom")),
            P(("tok", "atom")),
            P(("tok", "atom"), None),
            P(None, "tok", None),
            P(("tok", "atom"), None, None),
            P(),
            P(),
            P(),
            P(),
            P(),
            P(None, None, "tok"),
            P(),
            P("tok", None),
        ),
        out_specs=(P(("tok", "atom"), None), P(("tok", "atom"), None)),
        check_vma=False,
    )
```
